128 devices in a mesh: dp: 8 (over y, x_lo), tensor: 16 (over z, x_hi, core).
Axes of the slice: x: 4 (x_hi: 2, x_lo: 2; x = x_hi * 2 + x_lo), y: 4, z: 4, core: 2. Of those that a mesh axis runs over, the one named last changes fastest.
Arguments:
- tokens: bfloat16 [1280, 4096], P(('dp', 'tensor')), may hold values from -6 to 6
- grad_out: bfloat16 [1280, 4096], P(('dp', 'tensor')), may hold values from -6 to 6
- block_mask: int32 [32, 112], replicated, may hold values from 0 to 1, as said below
- gate_blocks: bfloat16 [2240, 128, 128], P('tensor'), may hold values from -0.125 to 0.125
- up_blocks: bfloat16 [2240, 128, 128], P('tensor'), may hold values from -0.125 to 0.125
- down_blocks: bfloat16 [2240, 128, 128], P('tensor'), may hold values from -0.0625 to 0.0625
Outputs:
- mixed: bfloat16 [1280, 4096], P(('dp', 'tensor'))
- grad_tokens: bfloat16 [1280, 4096], P(('dp', 'tensor'))
- grad_gate: bfloat16 [2240, 128, 128], P('tensor', 'dp')
- grad_up: bfloat16 [2240, 128, 128], P('tensor', 'dp')
- grad_down: bfloat16 [2240, 128, 128], P('tensor', 'dp')
The draws below stay inside these ranges and needn't reach their ends.
Inputs may be any that keep to these rules, and one draw needn't show every extreme that they name: `block_mask`: each shard of 7 consecutive hidden column blocks keeps at most 140 of its 224 blocks, and some shard keeps exactly 140; the same mask prunes all three projections.
All inputs are finite; a program needn't handle non-finite values.
Results may differ from the reference program's by a relative error of at most 0.023.
Values may be sent and summed in bfloat16 or wider, within the bound.
A program may use at most 192 MiB of HBM per device.

```python
import jax
import jax.numpy as jnp
from jax import lax

D = 4096
FF = 14336
BS = 128
RB = 32
CB = 7
BLK = 224
CAP = 140
GROUP = 160
TOKENS = 1280
N_DP = 8
N_TENSOR = 16


def draw_block_mask(key, part):
    key = jax.random.fold_in(key, 7)
    count_key, full_key, order_key = jax.random.split(key, 3)
    counts = jax.random.randint(count_key, (N_TENSOR,), max(1, BLK // 4), CAP + 1)
    fullest = jax.random.randint(full_key, (), 0, N_TENSOR)
    counts = jnp.where(jnp.arange(N_TENSOR) == fullest, CAP, counts)
    orders = jax.vmap(lambda sub_key: jax.random.permutation(sub_key, BLK))(jax.random.split(order_key, N_TENSOR))
    ranks = jnp.argsort(orders, axis=1)
    kept = (ranks < counts[:, None]).astype(jnp.int32)
    return kept.reshape(N_TENSOR, RB, CB).transpose(1, 0, 2).reshape(RB, N_TENSOR * CB)


def block_levels(own_key, extent, shards, least, top_value):
    def one(axis_at, shards_of):
        steps = jax.random.uniform(jax.random.fold_in(jax.random.fold_in(own_key, 6), axis_at), (shards_of,), jnp.float32, least / len(shards), top_value / len(shards))
        return jnp.repeat(jnp.exp(steps), extent[axis_at] // shards_of).reshape((-1,) + (1,) * (len(extent) - axis_at - 1))

    loudness = one(*shards[0])
    for cut in shards[1:]:
        loudness = loudness * one(*cut)
    return loudness


def normal_values(key, dims, spread, most, cuts=(), kind=jnp.bfloat16):
    values = jax.random.normal(key, dims, jnp.float32) * spread
    if len(cuts) > 0:
        values = block_levels(key, dims, cuts, -0.22, 0.18) * values
    return jnp.clip(values, min=-most, max=most).astype(kind)


def setup_inputs(seed: int = 0) -> dict:
    seeds = jax.random.split(jax.random.key(seed), 7)
    return {
        "tokens": normal_values(seeds[0], (TOKENS, D), 1.0, 6.0, ((0, 128),)),
        "grad_out": normal_values(seeds[1], (TOKENS, D), 1.0, 6.0, ((0, 128),)),
        "block_mask": draw_block_mask(jax.random.fold_in(seeds[6], 71), 0),
        "gate_blocks": normal_values(seeds[3], (N_TENSOR * CAP, BS, BS), (D // 2) ** -0.5, 0.125, ((0, 16),)),
        "up_blocks": normal_values(seeds[4], (N_TENSOR * CAP, BS, BS), (D // 2) ** -0.5, 0.125, ((0, 16),)),
        "down_blocks": normal_values(seeds[5], (N_TENSOR * CAP, BS, BS), (FF // 2) ** -0.5, 0.0625, ((0, 16),)),
    }


def kept_slots(block_mask):
    flags = block_mask.reshape(RB, N_TENSOR, CB).transpose(1, 0, 2).reshape(N_TENSOR, RB * CB)
    slot_index = jax.vmap(lambda flat_row: jnp.nonzero(flat_row, size=CAP, fill_value=0)[0].astype(jnp.int32))(flags)
    counts = jnp.sum(flags, axis=1).astype(jnp.int32)
    slot_live = jnp.arange(CAP, dtype=jnp.int32)[None, :] < counts[:, None]
    return slot_index // CB, slot_index % CB, slot_live


def shard_numbers():
    return jnp.broadcast_to(jnp.arange(N_TENSOR, dtype=jnp.int32)[:, None], (N_TENSOR, CAP))


def inward_dense(blocks, block_rows, block_cols, slot_live):
    pieces = blocks.reshape(N_TENSOR, CAP, BS, BS) * slot_live[:, :, None, None].astype(blocks.dtype)
    dense = jnp.zeros((N_TENSOR, RB, CB, BS, BS), blocks.dtype).at[shard_numbers(), block_rows, block_cols].add(pieces)
    return dense.transpose(1, 3, 0, 2, 4).reshape(D, FF)


def outward_dense(blocks, block_rows, block_cols, slot_live):
    pieces = blocks.reshape(N_TENSOR, CAP, BS, BS) * slot_live[:, :, None, None].astype(blocks.dtype)
    dense = jnp.zeros((N_TENSOR, CB, RB, BS, BS), blocks.dtype).at[shard_numbers(), block_cols, block_rows].add(pieces)
    return dense.transpose(0, 1, 3, 2, 4).reshape(FF, D)


def pick_inward(dense, block_rows, block_cols, slot_live):
    grid = dense.reshape(RB, BS, N_TENSOR, CB, BS).transpose(2, 0, 3, 1, 4)
    picked = grid[shard_numbers(), block_rows, block_cols]
    picked = jnp.where(slot_live[:, :, None, None], picked, jnp.zeros_like(picked))
    return picked.reshape(N_TENSOR * CAP, BS, BS)


def pick_outward(dense, block_rows, block_cols, slot_live):
    grid = dense.reshape(N_TENSOR, CB, BS, RB, BS).transpose(0, 1, 3, 2, 4)
    picked = grid[shard_numbers(), block_cols, block_rows]
    picked = jnp.where(slot_live[:, :, None, None], picked, jnp.zeros_like(picked))
    return picked.reshape(N_TENSOR * CAP, BS, BS)


def rounded(values):
    narrow = lax.optimization_barrier(values.astype(jnp.bfloat16))
    return narrow.astype(jnp.float32)


def reference(tokens, grad_out, block_mask, gate_blocks, up_blocks, down_blocks):
    block_rows, block_cols, slot_live = kept_slots(block_mask)
    w_gate = inward_dense(gate_blocks, block_rows, block_cols, slot_live)
    w_up = inward_dense(up_blocks, block_rows, block_cols, slot_live)
    w_down = outward_dense(down_blocks, block_rows, block_cols, slot_live)
    gate_pre = jnp.dot(tokens, w_gate, preferred_element_type=jnp.float32)
    up_pre = jnp.dot(tokens, w_up, preferred_element_type=jnp.float32)
    sigmoid_gate = jax.nn.sigmoid(gate_pre)
    silu_gate = gate_pre * sigmoid_gate
    hidden = (silu_gate * up_pre).astype(jnp.bfloat16)
    mixed = jnp.dot(hidden, w_down, preferred_element_type=jnp.float32).astype(jnp.bfloat16)
    grad_hidden = jnp.dot(grad_out, w_down.T, preferred_element_type=jnp.float32)
    grad_gate_act = (grad_hidden * up_pre * sigmoid_gate * (1.0 + gate_pre * (1.0 - sigmoid_gate))).astype(jnp.bfloat16)
    grad_up_act = (grad_hidden * silu_gate).astype(jnp.bfloat16)
    grad_tokens = (jnp.dot(grad_gate_act, w_gate.T, preferred_element_type=jnp.float32)
                   + jnp.dot(grad_up_act, w_up.T, preferred_element_type=jnp.float32)).astype(jnp.bfloat16)

    def accumulate(carry, group):
        tok_group, gate_group, up_group, hidden_group, cot_group = group
        gate_term = pick_inward(jnp.dot(tok_group.T, gate_group, preferred_element_type=jnp.float32), block_rows, block_cols, slot_live)
        up_term = pick_inward(jnp.dot(tok_group.T, up_group, preferred_element_type=jnp.float32), block_rows, block_cols, slot_live)
        down_term = pick_outward(jnp.dot(hidden_group.T, cot_group, preferred_element_type=jnp.float32), block_rows, block_cols, slot_live)
        return (carry[0] + rounded(gate_term), carry[1] + rounded(up_term), carry[2] + rounded(down_term)), None

    empty = jnp.zeros((N_TENSOR * CAP, BS, BS), jnp.float32)
    groups = (tokens.reshape(N_DP, GROUP, D), grad_gate_act.reshape(N_DP, GROUP, FF),
              grad_up_act.reshape(N_DP, GROUP, FF), hidden.reshape(N_DP, GROUP, FF),
              grad_out.reshape(N_DP, GROUP, D))
    totals, _ = lax.scan(accumulate, (empty, empty, empty), groups)
    return (mixed, grad_tokens, totals[0].astype(jnp.bfloat16), totals[1].astype(jnp.bfloat16),
            totals[2].astype(jnp.bfloat16))
```

```python
import functools

import jax
import jax.numpy as jnp
from jax import lax
from jax.experimental import pallas as pl
from jax.experimental.pallas import tpu as pltpu
from jax.sharding import PartitionSpec as P

MESH = pl.DeviceIdType.MESH
BF = jnp.bfloat16
F32 = jnp.float32


def nt_dot(a, b):
    return lax.dot_general(a, b, (((1,), (1,)), ((), ())), preferred_element_type=F32)


def tn_dot(a, b):
    return lax.dot_general(a, b, (((0,), (0,)), ((), ())), preferred_element_type=F32)


def kernel(
    dims,
    tok_ref, go_ref, slot_ref, kept_ref, gate_hbm, up_hbm, down_hbm,
    mixed_ref, gtok_ref, ggate_ref, gup_ref, gdown_ref,
    stage0, stage1, wgu, wd, chunks, rows, acts, hid, ggu, part, recv, cols, tokt,
    gblk, ublk, dblk, dsend, drecv, perm,
    load_sem, ag_send, ag_recv, fw_send,
    col_send, col_recv, colx_send, colx_recv,
    act_send, act_recv, rs_send, rs_recv, dn_send, dn_recv, loc_sem,
):
    ndp, nt, m, nh, rb, cb, cap = dims
    group = m * nt
    width = nh * 2048
    ds = width // ndp
    nchip = nt // 2
    rpd = rb // ndp
    d = lax.axis_index("dp")
    s = lax.axis_index("tensor")
    y, x = d // 2, d % 2
    chip, core = s // 2, s % 2
    ny = ndp // 2

    def peer(dd, ss):
        return (dd, ss)

    def rdma(src, dst, ssem, rsem, dev):
        return pltpu.make_async_remote_copy(
            src_ref=src, dst_ref=dst, send_sem=ssem, recv_sem=rsem,
            device_id=dev, device_id_type=MESH,
        )

    sib = chip * 2 + (1 - core)
    xp = y * 2 + (1 - x)
    yp = lax.rem(y + 1, ny) * 2 + x
    ym = lax.rem(y + ny - 1, ny) * 2 + x
    yp_o = lax.rem(y + 1, ny) * 2 + (1 - x)
    ym_o = lax.rem(y + ny - 1, ny) * 2 + (1 - x)
    y2 = lax.rem(y + 2, ny) * 2 + x
    y2_o = lax.rem(y + 2, ny) * 2 + (1 - x)

    load_g = pltpu.make_async_copy(gate_hbm, stage0.at[pl.ds(0, cap)], load_sem.at[0])
    load_u = pltpu.make_async_copy(up_hbm, stage1.at[pl.ds(0, cap)], load_sem.at[1])
    load_d = pltpu.make_async_copy(down_hbm, stage0.at[pl.ds(0, cap)], load_sem.at[2])
    barrier = pltpu.get_barrier_semaphore()
    for k in range(1, nt):
        pl.semaphore_signal(barrier, inc=1, device_id=peer(d, lax.rem(s + k, nt)), device_id_type=MESH)
    for k in range(1, ndp):
        pl.semaphore_signal(barrier, inc=1, device_id=peer(lax.rem(d + k, ndp), s), device_id_type=MESH)
    load_g.start()
    load_u.start()
    chunks[0, pl.ds(s * m, m)] = tok_ref[...]
    chunks[1, pl.ds(s * m, m)] = go_ref[...]
    stage0[cap] = jnp.zeros((128, 128), BF)
    stage1[cap] = jnp.zeros((128, 128), BF)
    ri = lax.broadcasted_iota(jnp.int32, (256, 256), 0)
    ci = lax.broadcasted_iota(jnp.int32, (256, 256), 1)
    perm[...] = jnp.where((ri // 16 == ci % 16) & (ri % 16 == ci // 16), 1.0, 0.0).astype(BF)
    pl.semaphore_wait(barrier, nt - 1 + ndp - 1)

    def chunk(src):
        return chunks.at[:, pl.ds(src * m, m)]

    def ag_copy(k):
        dst = lax.rem(chip + k, nchip) * 2 + core
        return rdma(chunk(s), chunk(s), ag_send.at[k], ag_recv.at[s], peer(d, dst))

    def fw_copy(k):
        src = lax.rem(chip + nchip - k, nchip) * 2 + core
        return rdma(chunk(src), chunk(src), fw_send.at[k], ag_recv.at[src], peer(d, sib))

    def ag_arrived(src):
        return rdma(chunk(src), chunk(src), ag_send.at[0], ag_recv.at[src], peer(d, sib))

    for k in range(1, nchip):
        ag_copy(k).start()
    fw_copy(0).start()

    def lay_inward(stage, lo):
        @pl.loop(0, rb)
        def _(r):
            for c in range(cb):
                blk = stage[slot_ref[r * cb + c]]
                for o in range(ndp):
                    wgu[c, pl.ds(pl.multiple_of(o * ds + r * 16, 16), 16), lo:lo + 128] = blk[o * 16:(o + 1) * 16]

    load_g.wait()
    lay_inward(stage0, 0)
    load_d.start()
    load_u.wait()
    lay_inward(stage1, 128)

    for k in range(1, nchip):
        ag_arrived(lax.rem(chip + nchip - k, nchip) * 2 + core).wait_recv()
        fw_copy(k).start()

    load_d.wait()

    @pl.loop(0, rb)
    def _(r):
        for c in range(cb):
            wd[c * 128:(c + 1) * 128, pl.ds(pl.multiple_of(r * 128, 128), 128)] = stage0[slot_ref[r * cb + c]]

    for k in range(nchip):
        ag_arrived(lax.rem(chip + nchip - k, nchip) * 2 + (1 - core)).wait_recv()

    pmat = perm[...]
    for a in range(2):
        @pl.loop(0, group // 16)
        def _(tb):
            t0 = pl.multiple_of(tb * 16, 16)
            for h in range(nh):
                mat = chunks[a, pl.ds(t0, 16), h].reshape(256, 128)
                out = jnp.dot(pmat, mat, preferred_element_type=F32).astype(BF)
                for j in range(16):
                    lo = (h * 16 + j) * 128
                    rows[a, pl.ds(t0, 16), lo:lo + 128] = out[j * 16:(j + 1) * 16]

    def col_slice(o):
        return rows.at[core, :, pl.ds(pl.multiple_of(o * ds, 128), ds)]

    def col_copy(k):
        dst = lax.rem(d + k, ndp)
        return rdma(col_slice(dst), cols.at[core, d], col_send.at[k], col_recv.at[d], peer(dst, s))

    def col_arrived(src):
        return rdma(cols.at[core, src], cols.at[core, src], col_send.at[0], col_recv.at[src], peer(d, sib))

    for k in range(1, ndp):
        col_copy(k).start()
    own_cols = pltpu.make_async_copy(col_slice(d), cols.at[core, d], loc_sem.at[0])
    own_cols.start()

    def act_copy(c, g, n, dst):
        return rdma(acts.at[c, g], acts.at[c, g], act_send.at[c, n], act_recv.at[c, g], peer(dst, s))

    def act_arrived(c, g):
        act_copy(c, g, 0, xp).wait_recv()

    @pl.loop(0, cb)
    def _(c):
        gu = jnp.dot(rows[0], wgu[c], preferred_element_type=F32)
        gh = nt_dot(rows[1], wd[pl.ds(pl.multiple_of(c * 128, 128), 128), :])
        gate, up = gu[:, :128], gu[:, 128:]
        sig = jax.nn.sigmoid(gate)
        silu = gate * sig
        hidden = (silu * up).astype(BF)
        gga = (gh * up * sig * (1.0 + gate * (1.0 - sig))).astype(BF)
        gua = (gh * silu).astype(BF)
        acts[c, d, :, 0:128] = gga
        acts[c, d, :, 128:256] = gua
        acts[c, d, :, 256:384] = hidden
        act_copy(c, d, 0, xp).start()
        act_copy(c, d, 1, yp).start()
        act_copy(c, d, 2, ym).start()
        ggu[:, pl.ds(pl.multiple_of(c * 256, 128), 128)] = gga
        ggu[:, pl.ds(pl.multiple_of(c * 256 + 128, 128), 128)] = gua
        hid[:, pl.ds(pl.multiple_of(c * 128, 128), 128)] = hidden

    for k in range(1, nchip):
        ag_copy(k).wait_send()
    for k in range(nchip):
        fw_copy(k).wait_send()

    @pl.loop(0, cb)
    def _(c):
        act_arrived(c, xp)
        act_copy(c, xp, 3, yp).start()
        act_copy(c, xp, 4, ym).start()

    step = min(512, width)

    @pl.loop(0, width // step)
    def _(n):
        lo = pl.multiple_of(n * step, step)
        part[0, :, pl.ds(lo, step)] = jnp.dot(
            hid[...], wd[:, pl.ds(lo, step)], preferred_element_type=F32
        ).astype(BF)
        wide = jnp.concatenate([wgu[c, pl.ds(lo, step), :] for c in range(cb)], axis=1)
        part[1, :, pl.ds(lo, step)] = nt_dot(ggu[...], wide).astype(BF)

    for a in range(2):
        @pl.loop(0, group // 16)
        def _(tb):
            t0 = pl.multiple_of(tb * 16, 16)
            for h in range(nh):
                mat = jnp.concatenate(
                    [part[a, pl.ds(t0, 16), (h * 16 + j) * 128:(h * 16 + j + 1) * 128] for j in range(16)],
                    axis=0,
                )
                out = jnp.dot(pmat, mat, preferred_element_type=F32).astype(BF)
                chunks[a, pl.ds(t0, 16), h] = out.reshape(16, 16, 128)

    def rs_copy(k):
        dst = lax.rem(s + k, nt)
        return rdma(chunk(dst), recv.at[:, s], rs_send.at[k], rs_recv.at[s], peer(d, dst))

    for k in range(1, nt):
        rs_copy(k).start()
    for a in range(2):
        recv[a, s] = chunks[a, pl.ds(s * m, m)]

    @pl.loop(0, cb)
    def _(c):
        act_arrived(c, ym)
        act_copy(c, ym, 5, yp).start()
        act_arrived(c, yp_o)
        act_copy(c, yp_o, 6, ym).start()

    own_cols.wait()
    for k in range(1, ndp):
        col_arrived(lax.rem(d + k, ndp)).wait_recv()
    colx = rdma(cols.at[core], cols.at[core], colx_send, colx_recv, peer(d, sib))
    colx.start()
    rdma(cols.at[1 - core], cols.at[1 - core], colx_send, colx_recv, peer(d, sib)).wait_recv()
    total = ndp * group
    tall = cols[0].reshape(total, ds)
    for q in range(total // 128):
        tokt[:, q * 128:(q + 1) * 128] = tall[q * 128:(q + 1) * 128].T

    def dn_copy(c, k):
        dst = lax.rem(d + k, ndp)
        return rdma(dsend.at[dst, c], drecv.at[d, c], dn_send.at[k], dn_recv.at[d], peer(dst, s))

    @pl.loop(0, cb)
    def _(c):
        for g in (ym_o, yp, y2, y2_o):
            act_arrived(c, g)
        down = tn_dot(acts[c, :, :, 256:384].reshape(total, 128), cols[1].reshape(total, ds)).astype(BF)
        for o in range(ndp):
            dsend[o, c] = down[o * 16:(o + 1) * 16]
        for k in range(1, ndp):
            dn_copy(c, k).start()
        drecv[d, c] = dsend[d, c]
        both = jnp.dot(
            tokt[...], acts[c, :, :, 0:256].reshape(total, 256), preferred_element_type=F32
        ).astype(BF)
        for r in range(rb):
            gblk[r * cb + c] = both[r * 16:(r + 1) * 16, :128]
            ublk[r * cb + c] = both[r * 16:(r + 1) * 16, 128:]

    zero = jnp.zeros((16, 128), BF)
    gblk[rb * cb] = zero
    ublk[rb * cb] = zero
    dblk[rb * cb] = zero

    @pl.loop(0, cap)
    def _(k):
        ggate_ref[k] = gblk[kept_ref[k]]
        gup_ref[k] = ublk[kept_ref[k]]

    for k in range(1, nt):
        src = lax.rem(s + k, nt)
        rdma(recv.at[:, src], recv.at[:, src], rs_send.at[0], rs_recv.at[src], peer(d, sib)).wait_recv()

    @pl.loop(0, m)
    def _(t):
        mixed_ref[t] = jnp.sum(recv[0, :, t].astype(F32), axis=0).astype(BF)
        gtok_ref[t] = jnp.sum(recv[1, :, t].astype(F32), axis=0).astype(BF)

    for k in range(1, ndp):
        src = lax.rem(d + k, ndp)
        rdma(drecv.at[src], drecv.at[src], dn_send.at[0], dn_recv.at[src], peer(d, sib)).wait_recv()
    for r in range(rb):
        for c in range(cb):
            lo = (r % rpd) * 128
            dblk[r * cb + c] = drecv[r // rpd, c, :, lo:lo + 128]

    @pl.loop(0, cap)
    def _(k):
        gdown_ref[k] = dblk[kept_ref[k]]

    for k in range(1, ndp):
        col_copy(k).wait_send()
        rdma(dsend.at[lax.rem(d + k, ndp)], drecv.at[d], dn_send.at[k], dn_recv.at[d], peer(d, sib)).wait_send()
    colx.wait_send()
    for k in range(1, nt):
        rs_copy(k).wait_send()

    @pl.loop(0, cb)
    def _(c):
        for n, g in enumerate((d, d, d, xp, xp, ym, yp_o)):
            act_copy(c, g, n, xp).wait_send()


def on_device(tokens, grad_out, block_mask, gate_blocks, up_blocks, down_blocks):
    nt = lax.axis_size("tensor")
    ndp = lax.axis_size("dp")
    shard = lax.axis_index("tensor")
    rb = block_mask.shape[0]
    cb = block_mask.shape[1] // nt
    cap = gate_blocks.shape[0]
    m, width = tokens.shape
    nh = width // 2048
    group = m * nt
    ds = width // ndp
    nb = rb * cb
    flags = lax.dynamic_slice_in_dim(block_mask, shard * cb, cb, 1).reshape(-1)
    pos = jnp.arange(nb, dtype=jnp.int32)
    upto = jnp.sum(jnp.where(pos[None, :] <= pos[:, None], flags[None, :], 0), axis=1)
    slot = jnp.where(flags > 0, upto - 1, cap)
    kept = jnp.sum((upto[None, :] <= jnp.arange(cap, dtype=jnp.int32)[:, None]).astype(jnp.int32), axis=1)

    tok = tokens.reshape(m, rb, ndp, 16).transpose(0, 2, 1, 3).reshape(m, nh, 16, 128)
    go = grad_out.reshape(m, nh, 16, 128)

    vm = pl.BlockSpec(memory_space=pltpu.VMEM)
    sm = pl.BlockSpec(memory_space=pltpu.SMEM)
    hb = pl.BlockSpec(memory_space=pl.ANY)
    dma = pltpu.SemaphoreType.DMA
    row_chunk = jax.ShapeDtypeStruct((m, nh, 16, 128), BF)
    grad = jax.ShapeDtypeStruct((cap, 16, 128), BF)
    mixed, gtok, ggate, gup, gdown = pl.pallas_call(
        functools.partial(kernel, (ndp, nt, m, nh, rb, cb, cap)),
        out_shape=(row_chunk, row_chunk, grad, grad, grad),
        in_specs=[vm, vm, sm, sm, hb, hb, hb],
        out_specs=[vm] * 5,
        scratch_shapes=[
            pltpu.VMEM((cap + 1, 128, 128), BF),
            pltpu.VMEM((cap + 1, 128, 128), BF),
            pltpu.VMEM((cb, width, 256), BF),
            pltpu.VMEM((cb * 128, width), BF),
            pltpu.VMEM((2, group, nh, 16, 128), BF),
            pltpu.VMEM((2, group, width), BF),
            pltpu.VMEM((cb, ndp, group, 384), BF),
            pltpu.VMEM((group, cb * 128), BF),
            pltpu.VMEM((group, cb * 256), BF),
            pltpu.VMEM((2, group, width), BF),
            pltpu.VMEM((2, nt, m, nh, 16, 128), BF),
            pltpu.VMEM((2, ndp, group, ds), BF),
            pltpu.VMEM((ds, ndp * group), BF),
            pltpu.VMEM((nb + 1, 16, 128), BF),
            pltpu.VMEM((nb + 1, 16, 128), BF),
            pltpu.VMEM((nb + 1, 16, 128), BF),
            pltpu.VMEM((ndp, cb, 16, ds), BF),
            pltpu.VMEM((ndp, cb, 16, ds), BF),
            pltpu.VMEM((256, 256), BF),
            dma((3,)),
            dma((nt,)),
            dma((nt,)),
            dma((nt,)),
            dma((ndp,)),
            dma((ndp,)),
            dma,
            dma,
            dma((cb, 7)),
            dma((cb, ndp)),
            dma((nt,)),
            dma((nt,)),
            dma((ndp,)),
            dma((ndp,)),
            dma((1,)),
        ],
        compiler_params=pltpu.CompilerParams(
            collective_id=0, has_side_effects=True, vmem_limit_bytes=64 * 1024 * 1024
        ),
    )(tok, go, slot, kept, gate_blocks, up_blocks, down_blocks)
    grad_tokens = gtok.reshape(m, ndp, rb, 16).transpose(0, 2, 1, 3).reshape(m, width)
    return mixed.reshape(m, width), grad_tokens, ggate, gup, gdown


def solution(mesh):
    rows = P(("dp", "tensor"), None)
    blocks = P("tensor", None, None)
    grads = P("tensor", "dp", None)
    return jax.shard_map(
        on_device,
        mesh=mesh,
        in_specs=(rows, rows, P(), blocks, blocks, blocks),
        out_specs=(rows, rows, grads, grads, grads),
        check_vma=False,
    )
```

```python
import functools

import jax
import jax.numpy as jnp
from jax import lax
from jax.experimental import pallas as pl
from jax.experimental.pallas import tpu as pltpu
from jax.sharding import PartitionSpec as P

MESH = pl.DeviceIdType.MESH
BF = jnp.bfloat16
F32 = jnp.float32


def nt_dot(a, b):
    return lax.dot_general(a, b, (((1,), (1,)), ((), ())), preferred_element_type=F32)


def tn_dot(a, b):
    return lax.dot_general(a, b, (((0,), (0,)), ((), ())), preferred_element_type=F32)


def swap_matrix(outer, inner):
    n = outer * inner
    o = lax.broadcasted_iota(jnp.int32, (n, n), 0)
    i = lax.broadcasted_iota(jnp.int32, (n, n), 1)
    hit = (o // outer == i % inner) & (o % outer == i // inner)
    return jnp.where(hit, 1.0, 0.0).astype(BF)


def move(a, b):
    return jnp.dot(a, b, preferred_element_type=F32).astype(BF)


def kernel(
    dims,
    tok_ref, go_ref, slot_ref, kept_ref, gate_hbm, up_hbm, down_hbm,
    mixed_ref, gtok_ref, ggate_ref, gup_ref, gdown_ref,
    stage0, stage1, wgu, wd, own16, chunks, rows, gus, acth, actg, hid, ggu, sibx, recv, fin,
    qsend, qrecv, craw, cols, tokt, gblk, ublk, dblk, dsend, drecv, perm,
    load_sem, ag_send, ag_recv, fw_send, q_send, q_recv, cg_send, cg_recv, cf_send,
    h_send, h_recv, g_send, g_recv, sib_send, sib_recv, rs_send, rs_recv, dn_send, dn_recv,
):
    ndp, nt, m, nh, rb, cb, cap = dims
    group = m * nt
    width = nh * 2048
    ds = width // ndp
    nj = ds // 128
    nchip = nt // 2
    rpd = rb // ndp
    cm = m * 2 * nj // 16
    total = ndp * group
    d = lax.axis_index("dp")
    s = lax.axis_index("tensor")
    y, x = d // 2, d % 2
    chip, core = s // 2, s % 2
    ny = ndp // 2

    def rdma(src, dst, ssem, rsem, dev):
        return pltpu.make_async_remote_copy(
            src_ref=src, dst_ref=dst, send_sem=ssem, recv_sem=rsem,
            device_id=dev, device_id_type=MESH,
        )

    sib = chip * 2 + (1 - core)
    xp = y * 2 + (1 - x)
    yp = lax.rem(y + 1, ny) * 2 + x
    ym = lax.rem(y + ny - 1, ny) * 2 + x
    yp_o = lax.rem(y + 1, ny) * 2 + (1 - x)
    ym_o = lax.rem(y + ny - 1, ny) * 2 + (1 - x)
    y2 = lax.rem(y + 2, ny) * 2 + x
    y2_o = lax.rem(y + 2, ny) * 2 + (1 - x)

    def chip_ahead(k):
        return lax.rem(chip + k, nchip)

    def chip_behind(k):
        return lax.rem(chip + nchip - k, nchip)

    load_g = pltpu.make_async_copy(gate_hbm, stage0.at[pl.ds(0, cap)], load_sem.at[0])
    load_u = pltpu.make_async_copy(up_hbm, stage1.at[pl.ds(0, cap)], load_sem.at[1])
    load_d = pltpu.make_async_copy(down_hbm, stage0.at[pl.ds(0, cap)], load_sem.at[2])
    barrier = pltpu.get_barrier_semaphore()
    for k in range(1, nt):
        pl.semaphore_signal(barrier, inc=1, device_id=(d, lax.rem(s + k, nt)), device_id_type=MESH)
    for k in range(1, ndp):
        pl.semaphore_signal(barrier, inc=1, device_id=(lax.rem(d + k, ndp), s), device_id_type=MESH)
    load_g.start()
    load_u.start()
    stage0[cap] = jnp.zeros((128, 128), BF)
    stage1[cap] = jnp.zeros((128, 128), BF)
    own16[...] = jnp.zeros_like(own16)
    fin[...] = jnp.zeros_like(fin)
    own16[0, 0:m, :] = tok_ref[...]
    own16[1, 0:m, :] = go_ref[...]
    perm[...] = swap_matrix(16, 16)

    for a in range(2):
        mat = jnp.concatenate(
            [
                jnp.concatenate(
                    [own16[a, :, (h * 16 + j) * 128:(h * 16 + j + 1) * 128] for j in range(16)], axis=0
                )
                for h in range(nh)
            ],
            axis=1,
        )
        out = move(perm[...], mat)
        for h in range(nh):
            chunks[a, pl.ds(s * m, m), h] = out[:, h * 128:(h + 1) * 128].reshape(16, 16, 128)[:m]
    pl.semaphore_wait(barrier, nt - 1 + ndp - 1)

    def chunk(a, src):
        return chunks.at[a, pl.ds(src * m, m)]

    def ag_copy(a, k):
        dst = chip_ahead(k) * 2 + core
        return rdma(chunk(a, s), chunk(a, s), ag_send.at[a, k], ag_recv.at[a, s], (d, dst))

    def fw_copy(a, k):
        src = chip_behind(k) * 2 + core
        return rdma(chunk(a, src), chunk(a, src), fw_send.at[a, k], ag_recv.at[a, src], (d, sib))

    def ag_arrived(a, src):
        rdma(chunk(a, src), chunk(a, src), ag_send.at[a, 0], ag_recv.at[a, src], (d, sib)).wait_recv()

    for a in range(2):
        for k in range(1, nchip):
            ag_copy(a, k).start()
        fw_copy(a, 0).start()

    def lay_inward(stage, lo):
        @pl.loop(0, rb)
        def _(r):
            for c in range(cb):
                wgu[c, pl.ds(pl.multiple_of(r * 128, 128), 128), lo:lo + 128] = stage[slot_ref[r * cb + c]]

    load_g.wait()
    lay_inward(stage0, 0)
    load_d.start()
    load_u.wait()
    lay_inward(stage1, 128)

    @pl.loop(0, ndp // 2)
    def _(pair):
        stack = jnp.concatenate(
            [own16[0, :, q * 1024:(q + 1) * 1024] for q in range(width // 1024)], axis=0
        )
        i = lax.broadcasted_iota(jnp.int32, (1024, 256), 0)
        o = lax.broadcasted_iota(jnp.int32, (1024, 256), 1) + pair * 256
        hit = (i // 128 == (o // 16) % 8) & ((i // 16) % 8 == o // 128) & (i % 16 == o % 16)
        toks = move(stack, jnp.where(hit, 1.0, 0.0).astype(BF))
        halves = []
        for w in range(2):
            base = pl.multiple_of((pair * 2 + w) * ds, 128)
            gos = jnp.concatenate(
                [own16[1, :, pl.ds(pl.multiple_of(base + j * 128, 128), 128)] for j in range(nj)], axis=0
            )
            halves.append(jnp.concatenate([toks[:, w * 128:(w + 1) * 128], gos], axis=0))
        out = move(swap_matrix(2 * nj, 16), jnp.concatenate(halves, axis=1))
        for w in range(2):
            qsend[pair * 2 + w] = out[0:cm * 16, w * 128:(w + 1) * 128].reshape(cm, 16, 128)

    def q_copy(k):
        dst = lax.rem(d + k, ndp)
        return rdma(qsend.at[dst], qrecv.at[d], q_send.at[k], q_recv.at[d], (dst, s))

    for k in range(1, ndp):
        q_copy(k).start()
    qrecv[d] = qsend[d]

    def forward(a):
        for k in range(1, nchip):
            ag_arrived(a, chip_behind(k) * 2 + core)
            fw_copy(a, k).start()

    def to_rows(a):
        @pl.loop(0, group // 16)
        def _(tb):
            t0 = pl.multiple_of(tb * 16, 16)
            mat = jnp.concatenate(
                [chunks[a, pl.ds(t0, 16), h].reshape(256, 128) for h in range(nh)], axis=1
            )
            out = move(perm[...], mat)
            for h in range(nh):
                for j in range(16):
                    lo = (h * 16 + j) * 128
                    rows[a, pl.ds(t0, 16), lo:lo + 128] = out[j * 16:(j + 1) * 16, h * 128:(h + 1) * 128]

    forward(0)
    for k in range(nchip):
        ag_arrived(0, chip_behind(k) * 2 + (1 - core))
    to_rows(0)

    def h_copy(c, g, n, dst):
        return rdma(acth.at[c, g], acth.at[c, g], h_send.at[c, n], h_recv.at[c, g], (dst, s))

    def g_copy(c, g, n, dst):
        return rdma(actg.at[c, g], actg.at[c, g], g_send.at[c, n], g_recv.at[c, g], (dst, s))

    @pl.loop(0, cb)
    def _(c):
        gu = jnp.dot(rows[0], wgu[c], preferred_element_type=F32)
        gus[c] = gu
        gate, up = gu[:, :128], gu[:, 128:]
        hidden = (gate * jax.nn.sigmoid(gate) * up).astype(BF)
        acth[c, d] = hidden
        h_copy(c, d, 0, xp).start()
        h_copy(c, d, 1, yp).start()
        h_copy(c, d, 2, ym).start()
        hid[:, pl.ds(pl.multiple_of(c * 128, 128), 128)] = hidden

    forward(1)
    load_d.wait()

    @pl.loop(0, rb)
    def _(r):
        for c in range(cb):
            wd[c * 128:(c + 1) * 128, pl.ds(pl.multiple_of(r * 128, 128), 128)] = stage0[slot_ref[r * cb + c]]

    for k in range(nchip):
        ag_arrived(1, chip_behind(k) * 2 + (1 - core))
    to_rows(1)

    @pl.loop(0, cb)
    def _(c):
        gh = nt_dot(rows[1], wd[pl.ds(pl.multiple_of(c * 128, 128), 128), :])
        gu = gus[c]
        gate, up = gu[:, :128], gu[:, 128:]
        sig = jax.nn.sigmoid(gate)
        gga = (gh * up * sig * (1.0 + gate * (1.0 - sig))).astype(BF)
        gua = (gh * (gate * sig)).astype(BF)
        actg[c, d, :, 0:128] = gga
        actg[c, d, :, 128:256] = gua
        g_copy(c, d, 0, xp).start()
        g_copy(c, d, 1, yp).start()
        g_copy(c, d, 2, ym).start()
        ggu[:, pl.ds(pl.multiple_of(c * 256, 128), 128)] = gga
        ggu[:, pl.ds(pl.multiple_of(c * 256 + 128, 128), 128)] = gua

    @pl.loop(0, cb)
    def _(c):
        h_copy(c, xp, 0, xp).wait_recv()
        h_copy(c, xp, 3, yp).start()
        h_copy(c, xp, 4, ym).start()
        h_copy(c, ym, 0, xp).wait_recv()
        h_copy(c, ym, 5, yp).start()

    for k in range(1, ndp):
        src = lax.rem(d + k, ndp)
        rdma(qrecv.at[src], qrecv.at[src], q_send.at[0], q_recv.at[src], (d, sib)).wait_recv()

    def craw_of(src):
        return craw.at[:, pl.ds(src * cm, cm)]

    def cg_copy(k):
        dst = chip_ahead(k) * 2 + core
        return rdma(qrecv, craw_of(s), cg_send.at[k], cg_recv.at[s], (d, dst))

    own_to_sib = rdma(qrecv, craw_of(s), cg_send.at[0], cg_recv.at[s], (d, sib))

    def cf_copy(k):
        src = chip_behind(k) * 2 + core
        return rdma(craw_of(src), craw_of(src), cf_send.at[k], cg_recv.at[src], (d, sib))

    def cg_arrived(src):
        rdma(craw_of(src), craw_of(src), cg_send.at[0], cg_recv.at[src], (d, sib)).wait_recv()

    for k in range(1, nchip):
        cg_copy(k).start()
    own_to_sib.start()
    for g in range(ndp):
        craw[g, pl.ds(s * cm, cm)] = qrecv[g]

    for a in range(2):
        for k in range(1, nchip):
            ag_copy(a, k).wait_send()
        for k in range(nchip):
            fw_copy(a, k).wait_send()
    step = min(512, width)

    def to_chunks(a):
        @pl.loop(0, group // 16)
        def _(tb):
            t0 = pl.multiple_of(tb * 16, 16)
            mat = jnp.concatenate(
                [
                    jnp.concatenate(
                        [
                            rows[a, pl.ds(t0, 16), (h * 16 + j) * 128:(h * 16 + j + 1) * 128]
                            for j in range(16)
                        ],
                        axis=0,
                    )
                    for h in range(nh)
                ],
                axis=1,
            )
            out = move(perm[...], mat)
            for h in range(nh):
                chunks[a, pl.ds(t0, 16), h] = out[:, h * 128:(h + 1) * 128].reshape(16, 16, 128)

    def sib_copy(a, q):
        return rdma(chunk(a, q * 2 + (1 - core)), sibx.at[a, q], sib_send.at[a, q], sib_recv.at[a, q], (d, sib))

    @pl.loop(0, width // step)
    def _(n):
        lo = pl.multiple_of(n * step, step)
        rows[0, :, pl.ds(lo, step)] = jnp.dot(
            hid[...], wd[:, pl.ds(lo, step)], preferred_element_type=F32
        ).astype(BF)

    to_chunks(0)
    for q in range(nchip):
        sib_copy(0, q).start()

    @pl.loop(0, width // step)
    def _(n):
        lo = pl.multiple_of(n * step, step)
        wide = jnp.concatenate([wgu[c, pl.ds(lo, step), :] for c in range(cb)], axis=1)
        rows[1, :, pl.ds(lo, step)] = nt_dot(ggu[...], wide).astype(BF)

    to_chunks(1)
    for q in range(nchip):
        sib_copy(1, q).start()

    @pl.loop(0, cb)
    def _(c):
        g_copy(c, xp, 0, xp).wait_recv()
        g_copy(c, xp, 3, yp).start()
        g_copy(c, xp, 4, ym).start()
        g_copy(c, ym, 0, xp).wait_recv()
        g_copy(c, ym, 5, yp).start()

    def rs_copy(a, k):
        q = chip_ahead(k)
        return rdma(
            chunk(a, q * 2 + core), recv.at[a, chip], rs_send.at[a, k], rs_recv.at[a, chip], (d, q * 2 + core)
        )

    for a in range(2):
        for q in range(nchip):
            sib_copy(a, q).wait_recv()
        for k in range(nchip):
            q = chip_ahead(k)
            mine = pl.ds((q * 2 + core) * m, m)
            both = (chunks[a, mine].astype(F32) + sibx[a, q].astype(F32)).astype(BF)
            if k == 0:
                recv[a, chip] = both
            else:
                chunks[a, mine] = both
                rs_copy(a, k).start()

    @pl.loop(0, cb)
    def _(c):
        h_copy(c, yp_o, 0, xp).wait_recv()
        h_copy(c, yp_o, 6, ym).start()

    for k in range(1, nchip):
        cg_arrived(chip_behind(k) * 2 + core)
        cf_copy(k).start()
    for k in range(nchip):
        cg_arrived(chip_behind(k) * 2 + (1 - core))

    @pl.loop(0, ndp // 2)
    def _(gp):
        for tb in range(group // 32):
            per = 32 * 2 * nj // 16
            mat = jnp.concatenate(
                [craw[gp * 2 + w, tb * per:(tb + 1) * per].reshape(per * 16, 128) for w in range(2)], axis=1
            )
            out = move(swap_matrix(32, 2 * nj), mat)
            for w in range(2):
                for a in range(2):
                    for j in range(nj):
                        lo = (a * nj + j) * 32
                        cols[a, gp * 2 + w, tb * 32:(tb + 1) * 32, j * 128:(j + 1) * 128] = (
                            out[lo:lo + 32, w * 128:(w + 1) * 128]
                        )

    tall = cols[0].reshape(total, ds)
    for q in range(total // 128):
        tokt[:, q * 128:(q + 1) * 128] = tall[q * 128:(q + 1) * 128].T

    @pl.loop(0, cb)
    def _(c):
        g_copy(c, yp_o, 0, xp).wait_recv()
        g_copy(c, yp_o, 6, ym).start()

    def dn_copy(c, k):
        dst = lax.rem(d + k, ndp)
        return rdma(dsend.at[dst, c], drecv.at[d, c], dn_send.at[k], dn_recv.at[d], (dst, s))

    @pl.loop(0, cb)
    def _(c):
        for g in (ym_o, yp, y2, y2_o):
            h_copy(c, g, 0, xp).wait_recv()
        down = tn_dot(acth[c].reshape(total, 128), cols[1].reshape(total, ds)).astype(BF)
        for o in range(ndp):
            dsend[o, c] = down[o * 16:(o + 1) * 16]
        for k in range(1, ndp):
            dn_copy(c, k).start()
        drecv[d, c] = dsend[d, c]

    for a, out_ref in ((0, mixed_ref), (1, gtok_ref)):
        for k in range(1, nchip):
            q = chip_ahead(k)
            rdma(recv.at[a, q], recv.at[a, q], rs_send.at[a, 0], rs_recv.at[a, q], (d, sib)).wait_recv()
        fin[0:m] = jnp.sum(recv[a].astype(F32), axis=0).astype(BF)
        mat = jnp.concatenate([fin[:, h].reshape(256, 128) for h in range(nh)], axis=1)
        out = move(perm[...], mat)
        for h in range(nh):
            for j in range(16):
                lo = (h * 16 + j) * 128
                out_ref[:, lo:lo + 128] = out[j * 16:j * 16 + m, h * 128:(h + 1) * 128]

    @pl.loop(0, cb)
    def _(c):
        for g in (ym_o, yp, y2, y2_o):
            g_copy(c, g, 0, xp).wait_recv()
        both = jnp.dot(tokt[...], actg[c].reshape(total, 256), preferred_element_type=F32).astype(BF)
        for r in range(rb):
            gblk[r * cb + c] = both[r * 16:(r + 1) * 16, :128]
            ublk[r * cb + c] = both[r * 16:(r + 1) * 16, 128:]

    zero = jnp.zeros((16, 128), BF)
    gblk[rb * cb] = zero
    ublk[rb * cb] = zero
    dblk[rb * cb] = zero

    for k in range(1, ndp):
        src = lax.rem(d + k, ndp)
        rdma(drecv.at[src], drecv.at[src], dn_send.at[0], dn_recv.at[src], (d, sib)).wait_recv()
    for r in range(rb):
        for c in range(cb):
            lo = (r % rpd) * 128
            dblk[r * cb + c] = drecv[r // rpd, c, :, lo:lo + 128]

    @pl.loop(0, cap)
    def _(k):
        ggate_ref[k] = gblk[kept_ref[k]]
        gup_ref[k] = ublk[kept_ref[k]]
        gdown_ref[k] = dblk[kept_ref[k]]

    for k in range(1, ndp):
        q_copy(k).wait_send()
        rdma(dsend.at[lax.rem(d + k, ndp)], drecv.at[d], dn_send.at[k], dn_recv.at[d], (d, sib)).wait_send()
    own_to_sib.wait_send()
    for k in range(1, nchip):
        cg_copy(k).wait_send()
        cf_copy(k).wait_send()
    for a in range(2):
        for q in range(nchip):
            sib_copy(a, q).wait_send()
        for k in range(1, nchip):
            rs_copy(a, k).wait_send()

    @pl.loop(0, cb)
    def _(c):
        for n, g in enumerate((d, d, d, xp, xp, ym, yp_o)):
            h_copy(c, g, n, xp).wait_send()
            g_copy(c, g, n, xp).wait_send()


def on_device(tokens, grad_out, block_mask, gate_blocks, up_blocks, down_blocks):
    nt = lax.axis_size("tensor")
    ndp = lax.axis_size("dp")
    shard = lax.axis_index("tensor")
    rb = block_mask.shape[0]
    cb = block_mask.shape[1] // nt
    cap = gate_blocks.shape[0]
    m, width = tokens.shape
    nh = width // 2048
    group = m * nt
    ds = width // ndp
    nb = rb * cb
    cm = m * 2 * (ds // 128) // 16
    flags = lax.dynamic_slice_in_dim(block_mask, shard * cb, cb, 1).reshape(-1)
    pos = jnp.arange(nb, dtype=jnp.int32)
    upto = jnp.sum(jnp.where(pos[None, :] <= pos[:, None], flags[None, :], 0), axis=1)
    slot = jnp.where(flags > 0, upto - 1, cap)
    kept = jnp.sum((upto[None, :] <= jnp.arange(cap, dtype=jnp.int32)[:, None]).astype(jnp.int32), axis=1)

    vm = pl.BlockSpec(memory_space=pltpu.VMEM)
    sm = pl.BlockSpec(memory_space=pltpu.SMEM)
    hb = pl.BlockSpec(memory_space=pl.ANY)
    dma = pltpu.SemaphoreType.DMA
    own_rows = jax.ShapeDtypeStruct((m, width), BF)
    grad = jax.ShapeDtypeStruct((cap, 16, 128), BF)
    return pl.pallas_call(
        functools.partial(kernel, (ndp, nt, m, nh, rb, cb, cap)),
        out_shape=(own_rows, own_rows, grad, grad, grad),
        in_specs=[vm, vm, sm, sm, hb, hb, hb],
        out_specs=[vm] * 5,
        scratch_shapes=[
            pltpu.VMEM((cap + 1, 128, 128), BF),
            pltpu.VMEM((cap + 1, 128, 128), BF),
            pltpu.VMEM((cb, width, 256), BF),
            pltpu.VMEM((cb * 128, width), BF),
            pltpu.VMEM((2, 16, width), BF),
            pltpu.VMEM((2, group, nh, 16, 128), BF),
            pltpu.VMEM((2, group, width), BF),
            pltpu.VMEM((cb, group, 256), F32),
            pltpu.VMEM((cb, ndp, group, 128), BF),
            pltpu.VMEM((cb, ndp, group, 256), BF),
            pltpu.VMEM((group, cb * 128), BF),
            pltpu.VMEM((group, cb * 256), BF),
            pltpu.VMEM((2, nt // 2, m, nh, 16, 128), BF),
            pltpu.VMEM((2, nt // 2, m, nh, 16, 128), BF),
            pltpu.VMEM((16, nh, 16, 128), BF),
            pltpu.VMEM((ndp, cm, 16, 128), BF),
            pltpu.VMEM((ndp, cm, 16, 128), BF),
            pltpu.VMEM((ndp, nt * cm, 16, 128), BF),
            pltpu.VMEM((2, ndp, group, ds), BF),
            pltpu.VMEM((ds, ndp * group), BF),
            pltpu.VMEM((nb + 1, 16, 128), BF),
            pltpu.VMEM((nb + 1, 16, 128), BF),
            pltpu.VMEM((nb + 1, 16, 128), BF),
            pltpu.VMEM((ndp, cb, 16, ds), BF),
            pltpu.VMEM((ndp, cb, 16, ds), BF),
            pltpu.VMEM((256, 256), BF),
            dma((3,)),
            dma((2, nt // 2)),
            dma((2, nt)),
            dma((2, nt // 2)),
            dma((ndp,)),
            dma((ndp,)),
            dma((nt // 2,)),
            dma((nt,)),
            dma((nt // 2,)),
            dma((cb, 7)),
            dma((cb, ndp)),
            dma((cb, 7)),
            dma((cb, ndp)),
            dma((2, nt // 2)),
            dma((2, nt // 2)),
            dma((2, nt // 2)),
            dma((2, nt // 2)),
            dma((ndp,)),
            dma((ndp,)),
        ],
        compiler_params=pltpu.CompilerParams(
            collective_id=0, has_side_effects=True, vmem_limit_bytes=64 * 1024 * 1024
        ),
    )(tokens, grad_out, slot, kept, gate_blocks, up_blocks, down_blocks)


def solution(mesh):
    rows = P(("dp", "tensor"), None)
    blocks = P("tensor", None, None)
    grads = P("tensor", "dp", None)
    return jax.shard_map(
        on_device,
        mesh=mesh,
        in_specs=(rows, rows, P(), blocks, blocks, blocks),
        out_specs=(rows, rows, grads, grads, grads),
        check_vma=False,
    )
```

```python
import functools

import jax
import jax.numpy as jnp
from jax import lax
from jax.experimental import pallas as pl
from jax.experimental.pallas import tpu as pltpu
from jax.sharding import PartitionSpec as P

MESH = pl.DeviceIdType.MESH
BF = jnp.bfloat16
F32 = jnp.float32


def nt_dot(a, b):
    return lax.dot_general(a, b, (((1,), (1,)), ((), ())), preferred_element_type=F32)


def tn_dot(a, b):
    return lax.dot_general(a, b, (((0,), (0,)), ((), ())), preferred_element_type=F32)


def swap_matrix(outer, inner):
    n = outer * inner
    o = lax.broadcasted_iota(jnp.int32, (n, n), 0)
    i = lax.broadcasted_iota(jnp.int32, (n, n), 1)
    hit = (o // outer == i % inner) & (o % outer == i // inner)
    return jnp.where(hit, 1.0, 0.0).astype(BF)


def move(a, b):
    return jnp.dot(a, b, preferred_element_type=F32).astype(BF)


def kernel(
    dims,
    tok_ref, go_ref, slot_ref, kept_ref, gate_hbm, up_hbm, down_hbm,
    mixed_ref, gtok_ref, ggate_ref, gup_ref, gdown_ref,
    stage0, stage1, wgu, wd, own16, chunks, rows, gus, acth, actg, hid, ggu, sibx, recv, fin,
    qsend, qrecv, craw, cols, tokt, gblk, ublk, dblk, dsend, drecv, perm,
    load_sem, ag_send, ag_recv, fw_send, q_send, q_recv, cg_send, cg_recv, cf_send,
    h_send, h_recv, g_send, g_recv, sib_send, sib_recv, rs_send, rs_recv, dn_send, dn_recv,
):
    ndp, nt, m, nh, rb, cb, cap = dims
    group = m * nt
    width = nh * 2048
    ds = width // ndp
    nj = ds // 128
    nchip = nt // 2
    nz = nchip // 2
    rpd = rb // ndp
    cm = m * 2 * nj // 16
    total = ndp * group
    d = lax.axis_index("dp")
    s = lax.axis_index("tensor")
    y, x = d // 2, d % 2
    chip, core = s // 2, s % 2
    z, xh = chip // 2, chip % 2
    ny = ndp // 2

    def rdma(src, dst, ssem, rsem, dev):
        return pltpu.make_async_remote_copy(
            src_ref=src, dst_ref=dst, send_sem=ssem, recv_sem=rsem,
            device_id=dev, device_id_type=MESH,
        )

    sib = chip * 2 + (1 - core)
    xp = y * 2 + (1 - x)
    yp = lax.rem(y + 1, ny) * 2 + x
    ym = lax.rem(y + ny - 1, ny) * 2 + x
    yp_o = lax.rem(y + 1, ny) * 2 + (1 - x)
    ym_o = lax.rem(y + ny - 1, ny) * 2 + (1 - x)
    y2 = lax.rem(y + 2, ny) * 2 + x
    y2_o = lax.rem(y + 2, ny) * 2 + (1 - x)

    def chip_ahead(k):
        return lax.rem(chip + k, nchip)

    def chip_behind(k):
        return lax.rem(chip + nchip - k, nchip)

    load_g = pltpu.make_async_copy(gate_hbm, stage0.at[pl.ds(0, cap)], load_sem.at[0])
    load_u = pltpu.make_async_copy(up_hbm, stage1.at[pl.ds(0, cap)], load_sem.at[1])
    load_d = pltpu.make_async_copy(down_hbm, stage0.at[pl.ds(0, cap)], load_sem.at[2])
    barrier = pltpu.get_barrier_semaphore()
    for k in range(1, nt):
        pl.semaphore_signal(barrier, inc=1, device_id=(d, lax.rem(s + k, nt)), device_id_type=MESH)
    for k in range(1, ndp):
        pl.semaphore_signal(barrier, inc=1, device_id=(lax.rem(d + k, ndp), s), device_id_type=MESH)
    load_g.start()
    load_u.start()
    stage0[cap] = jnp.zeros((128, 128), BF)
    stage1[cap] = jnp.zeros((128, 128), BF)
    own16[...] = jnp.zeros_like(own16)
    fin[...] = jnp.zeros_like(fin)
    own16[0, 0:m, :] = tok_ref[...]
    own16[1, 0:m, :] = go_ref[...]
    perm[...] = swap_matrix(16, 16)

    for a in range(2):
        mat = jnp.concatenate(
            [
                jnp.concatenate(
                    [own16[a, :, (h * 16 + j) * 128:(h * 16 + j + 1) * 128] for j in range(16)], axis=0
                )
                for h in range(nh)
            ],
            axis=1,
        )
        out = move(perm[...], mat)
        for h in range(nh):
            chunks[a, pl.ds(s * m, m), h] = out[:, h * 128:(h + 1) * 128].reshape(16, 16, 128)[:m]
    pl.semaphore_wait(barrier, nt - 1 + ndp - 1)

    def chunk(a, src):
        return chunks.at[a, pl.ds(src * m, m)]

    def ag_copy(a, k):
        dst = chip_ahead(k) * 2 + core
        return rdma(chunk(a, s), chunk(a, s), ag_send.at[a, k], ag_recv.at[a, s], (d, dst))

    def fw_copy(a, k):
        src = chip_behind(k) * 2 + core
        return rdma(chunk(a, src), chunk(a, src), fw_send.at[a, k], ag_recv.at[a, src], (d, sib))

    def ag_arrived(a, src):
        rdma(chunk(a, src), chunk(a, src), ag_send.at[a, 0], ag_recv.at[a, src], (d, sib)).wait_recv()

    def send_own(a):
        for k in range(1, nchip):
            ag_copy(a, k).start()
        fw_copy(a, 0).start()

    send_own(0)

    def lay_inward(stage, lo):
        @pl.loop(0, rb)
        def _(r):
            for c in range(cb):
                wgu[c, pl.ds(pl.multiple_of(r * 128, 128), 128), lo:lo + 128] = stage[slot_ref[r * cb + c]]

    load_g.wait()
    lay_inward(stage0, 0)
    load_d.start()
    load_u.wait()
    send_own(1)
    lay_inward(stage1, 128)

    @pl.loop(0, ndp // 2)
    def _(pair):
        stack = jnp.concatenate(
            [own16[0, :, q * 1024:(q + 1) * 1024] for q in range(width // 1024)], axis=0
        )
        i = lax.broadcasted_iota(jnp.int32, (1024, 256), 0)
        o = lax.broadcasted_iota(jnp.int32, (1024, 256), 1) + pair * 256
        hit = (i // 128 == (o // 16) % 8) & ((i // 16) % 8 == o // 128) & (i % 16 == o % 16)
        toks = move(stack, jnp.where(hit, 1.0, 0.0).astype(BF))
        halves = []
        for w in range(2):
            base = pl.multiple_of((pair * 2 + w) * ds, 128)
            gos = jnp.concatenate(
                [own16[1, :, pl.ds(pl.multiple_of(base + j * 128, 128), 128)] for j in range(nj)], axis=0
            )
            halves.append(jnp.concatenate([toks[:, w * 128:(w + 1) * 128], gos], axis=0))
        out = move(swap_matrix(2 * nj, 16), jnp.concatenate(halves, axis=1))
        for w in range(2):
            qsend[pair * 2 + w] = out[0:cm * 16, w * 128:(w + 1) * 128].reshape(cm, 16, 128)

    def q_copy(k):
        dst = lax.rem(d + k, ndp)
        return rdma(qsend.at[dst], qrecv.at[d], q_send.at[k], q_recv.at[d], (dst, s))

    for k in range(1, ndp):
        q_copy(k).start()
    qrecv[d] = qsend[d]

    def forward(a):
        for k in range(1, nchip):
            ag_arrived(a, chip_behind(k) * 2 + core)
            fw_copy(a, k).start()

    def to_rows(a):
        @pl.loop(0, group // 16)
        def _(tb):
            t0 = pl.multiple_of(tb * 16, 16)
            mat = jnp.concatenate(
                [chunks[a, pl.ds(t0, 16), h].reshape(256, 128) for h in range(nh)], axis=1
            )
            out = move(perm[...], mat)
            for h in range(nh):
                for j in range(16):
                    lo = (h * 16 + j) * 128
                    rows[a, pl.ds(t0, 16), lo:lo + 128] = out[j * 16:(j + 1) * 16, h * 128:(h + 1) * 128]

    load_d.wait()

    @pl.loop(0, rb)
    def _(r):
        for c in range(cb):
            wd[c * 128:(c + 1) * 128, pl.ds(pl.multiple_of(r * 128, 128), 128)] = stage0[slot_ref[r * cb + c]]

    forward(0)
    for k in range(nchip):
        ag_arrived(0, chip_behind(k) * 2 + (1 - core))
    to_rows(0)

    def h_copy(c, g, n, dst):
        return rdma(acth.at[c, g], acth.at[c, g], h_send.at[c, n], h_recv.at[c, g], (dst, s))

    def g_copy(c, g, n, dst):
        return rdma(actg.at[c, g], actg.at[c, g], g_send.at[c, n], g_recv.at[c, g], (dst, s))

    @pl.loop(0, cb)
    def _(c):
        gu = jnp.dot(rows[0], wgu[c], preferred_element_type=F32)
        gus[c] = gu
        gate, up = gu[:, :128], gu[:, 128:]
        hidden = (gate * jax.nn.sigmoid(gate) * up).astype(BF)
        acth[c, d] = hidden
        h_copy(c, d, 0, xp).start()
        h_copy(c, d, 1, yp).start()
        h_copy(c, d, 2, ym).start()
        hid[:, pl.ds(pl.multiple_of(c * 128, 128), 128)] = hidden

    forward(1)
    for k in range(nchip):
        ag_arrived(1, chip_behind(k) * 2 + (1 - core))

    for k in range(1, ndp):
        src = lax.rem(d + k, ndp)
        rdma(qrecv.at[src], qrecv.at[src], q_send.at[0], q_recv.at[src], (d, sib)).wait_recv()

    def craw_of(src):
        return craw.at[:, pl.ds(src * cm, cm)]

    def at(kz, other, cr):
        along = 1 - xh if other else xh
        return (lax.rem(z + kz, nz) * 2 + along) * 2 + cr

    def cg_copy(n, dst):
        return rdma(qrecv, craw_of(s), cg_send.at[n], cg_recv.at[s], (d, dst))

    def cz_copy(k):
        src = at(0, True, core)
        return rdma(craw_of(src), craw_of(src), cg_send.at[nz + k], cg_recv.at[src], (d, at(k, False, core)))

    def cf_copy(k, other):
        src = at(k, other, core)
        return rdma(craw_of(src), craw_of(src), cf_send.at[k, other], cg_recv.at[src], (d, sib))

    def cg_arrived(src):
        rdma(craw_of(src), craw_of(src), cg_send.at[0], cg_recv.at[src], (d, sib)).wait_recv()

    cg_copy(0, sib).start()
    cg_copy(nz, at(0, True, core)).start()
    for k in range(1, nz):
        cg_copy(k, at(k, False, core)).start()
    for g in range(ndp):
        craw[g, pl.ds(s * cm, cm)] = qrecv[g]

    to_rows(1)

    @pl.loop(0, cb)
    def _(c):
        gh = nt_dot(rows[1], wd[pl.ds(pl.multiple_of(c * 128, 128), 128), :])
        gu = gus[c]
        gate, up = gu[:, :128], gu[:, 128:]
        sig = jax.nn.sigmoid(gate)
        gga = (gh * up * sig * (1.0 + gate * (1.0 - sig))).astype(BF)
        gua = (gh * (gate * sig)).astype(BF)
        actg[c, d, :, 0:128] = gga
        actg[c, d, :, 128:256] = gua
        g_copy(c, d, 0, xp).start()
        g_copy(c, d, 1, yp).start()
        g_copy(c, d, 2, ym).start()
        ggu[:, pl.ds(pl.multiple_of(c * 256, 128), 128)] = gga
        ggu[:, pl.ds(pl.multiple_of(c * 256 + 128, 128), 128)] = gua

    for a in range(2):
        for k in range(1, nchip):
            ag_copy(a, k).wait_send()
        for k in range(nchip):
            fw_copy(a, k).wait_send()
    step = min(512, width)

    def to_chunks(a):
        @pl.loop(0, group // 16)
        def _(tb):
            t0 = pl.multiple_of(tb * 16, 16)
            mat = jnp.concatenate(
                [
                    jnp.concatenate(
                        [
                            rows[a, pl.ds(t0, 16), (h * 16 + j) * 128:(h * 16 + j + 1) * 128]
                            for j in range(16)
                        ],
                        axis=0,
                    )
                    for h in range(nh)
                ],
                axis=1,
            )
            out = move(perm[...], mat)
            for h in range(nh):
                chunks[a, pl.ds(t0, 16), h] = out[:, h * 128:(h + 1) * 128].reshape(16, 16, 128)

    def sib_copy(a, q):
        return rdma(chunk(a, q * 2 + (1 - core)), sibx.at[a, q], sib_send.at[a, q], sib_recv.at[a, q], (d, sib))

    @pl.loop(0, cb)
    def _(c):
        h_copy(c, xp, 0, xp).wait_recv()
        h_copy(c, xp, 4, ym).start()
        h_copy(c, xp, 3, yp).start()

    cg_arrived(at(0, True, core))
    for k in range(1, nz):
        cz_copy(k).start()
    cf_copy(0, 1).start()

    @pl.loop(0, width // step)
    def _(n):
        lo = pl.multiple_of(n * step, step)
        rows[0, :, pl.ds(lo, step)] = jnp.dot(
            hid[...], wd[:, pl.ds(lo, step)], preferred_element_type=F32
        ).astype(BF)

    to_chunks(0)
    for q in range(nchip):
        sib_copy(0, q).start()

    @pl.loop(0, cb)
    def _(c):
        h_copy(c, ym, 0, xp).wait_recv()
        h_copy(c, ym, 5, yp).start()

    @pl.loop(0, width // step)
    def _(n):
        lo = pl.multiple_of(n * step, step)
        wide = jnp.concatenate([wgu[c, pl.ds(lo, step), :] for c in range(cb)], axis=1)
        rows[1, :, pl.ds(lo, step)] = nt_dot(ggu[...], wide).astype(BF)

    @pl.loop(0, cb)
    def _(c):
        g_copy(c, xp, 0, xp).wait_recv()
        g_copy(c, xp, 4, ym).start()
        g_copy(c, xp, 3, yp).start()

    to_chunks(1)
    for q in range(nchip):
        sib_copy(1, q).start()

    @pl.loop(0, cb)
    def _(c):
        h_copy(c, yp_o, 0, xp).wait_recv()
        h_copy(c, yp_o, 6, ym).start()

    def rs_copy(a, k):
        q = chip_ahead(k)
        return rdma(
            chunk(a, q * 2 + core), recv.at[a, chip], rs_send.at[a, k], rs_recv.at[a, chip], (d, q * 2 + core)
        )

    for a in range(2):
        for q in range(nchip):
            sib_copy(a, q).wait_recv()
        for k in range(nchip):
            q = chip_ahead(k)
            mine = pl.ds((q * 2 + core) * m, m)
            both = (chunks[a, mine].astype(F32) + sibx[a, q].astype(F32)).astype(BF)
            if k == 0:
                recv[a, chip] = both
            else:
                chunks[a, mine] = both
                rs_copy(a, k).start()

    @pl.loop(0, cb)
    def _(c):
        g_copy(c, ym, 0, xp).wait_recv()
        g_copy(c, ym, 5, yp).start()

    for k in range(1, nz):
        for other in range(2):
            cg_arrived(at(k, other, core))
            cf_copy(k, other).start()
    for k in range(nz):
        for other in range(2):
            cg_arrived(at(k, other, 1 - core))

    @pl.loop(0, ndp // 2)
    def _(gp):
        for tb in range(group // 32):
            per = 32 * 2 * nj // 16
            mat = jnp.concatenate(
                [craw[gp * 2 + w, tb * per:(tb + 1) * per].reshape(per * 16, 128) for w in range(2)], axis=1
            )
            out = move(swap_matrix(32, 2 * nj), mat)
            for w in range(2):
                for a in range(2):
                    for j in range(nj):
                        lo = (a * nj + j) * 32
                        cols[a, gp * 2 + w, tb * 32:(tb + 1) * 32, j * 128:(j + 1) * 128] = (
                            out[lo:lo + 32, w * 128:(w + 1) * 128]
                        )

    tall = cols[0].reshape(total, ds)
    for q in range(total // 128):
        tokt[:, q * 128:(q + 1) * 128] = tall[q * 128:(q + 1) * 128].T

    def dn_copy(c, k):
        dst = lax.rem(d + k, ndp)
        return rdma(dsend.at[dst, c], drecv.at[d, c], dn_send.at[k], dn_recv.at[d], (dst, s))

    @pl.loop(0, cb)
    def _(c):
        for g in (ym_o, yp, y2, y2_o):
            h_copy(c, g, 0, xp).wait_recv()
        down = tn_dot(acth[c].reshape(total, 128), cols[1].reshape(total, ds)).astype(BF)
        for o in range(ndp):
            dsend[o, c] = down[o * 16:(o + 1) * 16]
        for k in range(1, ndp):
            dn_copy(c, k).start()
        drecv[d, c] = dsend[d, c]

    @pl.loop(0, cb)
    def _(c):
        g_copy(c, yp_o, 0, xp).wait_recv()
        g_copy(c, yp_o, 6, ym).start()

    for a, out_ref in ((0, mixed_ref), (1, gtok_ref)):
        for k in range(1, nchip):
            q = chip_ahead(k)
            rdma(recv.at[a, q], recv.at[a, q], rs_send.at[a, 0], rs_recv.at[a, q], (d, sib)).wait_recv()
        fin[0:m] = jnp.sum(recv[a].astype(F32), axis=0).astype(BF)
        mat = jnp.concatenate([fin[:, h].reshape(256, 128) for h in range(nh)], axis=1)
        out = move(perm[...], mat)
        for h in range(nh):
            for j in range(16):
                lo = (h * 16 + j) * 128
                out_ref[:, lo:lo + 128] = out[j * 16:j * 16 + m, h * 128:(h + 1) * 128]

    @pl.loop(0, cb)
    def _(c):
        for g in (ym_o, yp, y2, y2_o):
            g_copy(c, g, 0, xp).wait_recv()
        both = jnp.dot(tokt[...], actg[c].reshape(total, 256), preferred_element_type=F32).astype(BF)
        for r in range(rb):
            gblk[r * cb + c] = both[r * 16:(r + 1) * 16, :128]
            ublk[r * cb + c] = both[r * 16:(r + 1) * 16, 128:]

    zero = jnp.zeros((16, 128), BF)
    gblk[rb * cb] = zero
    ublk[rb * cb] = zero
    dblk[rb * cb] = zero

    for k in range(1, ndp):
        src = lax.rem(d + k, ndp)
        rdma(drecv.at[src], drecv.at[src], dn_send.at[0], dn_recv.at[src], (d, sib)).wait_recv()
    for r in range(rb):
        for c in range(cb):
            lo = (r % rpd) * 128
            dblk[r * cb + c] = drecv[r // rpd, c, :, lo:lo + 128]

    @pl.loop(0, cap)
    def _(k):
        ggate_ref[k] = gblk[kept_ref[k]]
        gup_ref[k] = ublk[kept_ref[k]]
        gdown_ref[k] = dblk[kept_ref[k]]

    for k in range(1, ndp):
        q_copy(k).wait_send()
        rdma(dsend.at[lax.rem(d + k, ndp)], drecv.at[d], dn_send.at[k], dn_recv.at[d], (d, sib)).wait_send()
    cg_copy(0, sib).wait_send()
    cg_copy(nz, sib).wait_send()
    cf_copy(0, 1).wait_send()
    for k in range(1, nz):
        cg_copy(k, sib).wait_send()
        cz_copy(k).wait_send()
        for other in range(2):
            cf_copy(k, other).wait_send()
    for a in range(2):
        for q in range(nchip):
            sib_copy(a, q).wait_send()
        for k in range(1, nchip):
            rs_copy(a, k).wait_send()

    @pl.loop(0, cb)
    def _(c):
        for n, g in enumerate((d, d, d, xp, xp, ym, yp_o)):
            h_copy(c, g, n, xp).wait_send()
            g_copy(c, g, n, xp).wait_send()


def hand_out(n, *refs):
    sems = refs[-1]
    copies = [pltpu.make_async_copy(refs[i], refs[n + i], sems.at[i]) for i in range(n)]
    for copy in copies:
        copy.start()
    for copy in copies:
        copy.wait()


def on_device(tokens, grad_out, block_mask, gate_blocks, up_blocks, down_blocks):
    nt = lax.axis_size("tensor")
    ndp = lax.axis_size("dp")
    shard = lax.axis_index("tensor")
    rb = block_mask.shape[0]
    cb = block_mask.shape[1] // nt
    cap = gate_blocks.shape[0]
    m, width = tokens.shape
    nh = width // 2048
    group = m * nt
    ds = width // ndp
    nb = rb * cb
    cm = m * 2 * (ds // 128) // 16
    flags = lax.dynamic_slice_in_dim(block_mask, shard * cb, cb, 1).reshape(-1)
    pos = jnp.arange(nb, dtype=jnp.int32)
    upto = jnp.sum(jnp.where(pos[None, :] <= pos[:, None], flags[None, :], 0), axis=1)
    slot = jnp.where(flags > 0, upto - 1, cap)
    kept = jnp.sum((upto[None, :] <= jnp.arange(cap, dtype=jnp.int32)[:, None]).astype(jnp.int32), axis=1)

    vm = pl.BlockSpec(memory_space=pltpu.VMEM)
    sm = pl.BlockSpec(memory_space=pltpu.SMEM)
    hb = pl.BlockSpec(memory_space=pl.ANY)
    dma = pltpu.SemaphoreType.DMA
    own_rows = jax.ShapeDtypeStruct((m, width), BF)
    grad = jax.ShapeDtypeStruct((cap, 16, 128), BF)
    results = pl.pallas_call(
        functools.partial(kernel, (ndp, nt, m, nh, rb, cb, cap)),
        out_shape=(own_rows, own_rows, grad, grad, grad),
        in_specs=[vm, vm, sm, sm, hb, hb, hb],
        out_specs=[vm] * 5,
        scratch_shapes=[
            pltpu.VMEM((cap + 1, 128, 128), BF),
            pltpu.VMEM((cap + 1, 128, 128), BF),
            pltpu.VMEM((cb, width, 256), BF),
            pltpu.VMEM((cb * 128, width), BF),
            pltpu.VMEM((2, 16, width), BF),
            pltpu.VMEM((2, group, nh, 16, 128), BF),
            pltpu.VMEM((2, group, width), BF),
            pltpu.VMEM((cb, group, 256), F32),
            pltpu.VMEM((cb, ndp, group, 128), BF),
            pltpu.VMEM((cb, ndp, group, 256), BF),
            pltpu.VMEM((group, cb * 128), BF),
            pltpu.VMEM((group, cb * 256), BF),
            pltpu.VMEM((2, nt // 2, m, nh, 16, 128), BF),
            pltpu.VMEM((2, nt // 2, m, nh, 16, 128), BF),
            pltpu.VMEM((16, nh, 16, 128), BF),
            pltpu.VMEM((ndp, cm, 16, 128), BF),
            pltpu.VMEM((ndp, cm, 16, 128), BF),
            pltpu.VMEM((ndp, nt * cm, 16, 128), BF),
            pltpu.VMEM((2, ndp, group, ds), BF),
            pltpu.VMEM((ds, ndp * group), BF),
            pltpu.VMEM((nb + 1, 16, 128), BF),
            pltpu.VMEM((nb + 1, 16, 128), BF),
            pltpu.VMEM((nb + 1, 16, 128), BF),
            pltpu.VMEM((ndp, cb, 16, ds), BF),
            pltpu.VMEM((ndp, cb, 16, ds), BF),
            pltpu.VMEM((256, 256), BF),
            dma((3,)),
            dma((2, nt // 2)),
            dma((2, nt)),
            dma((2, nt // 2)),
            dma((ndp,)),
            dma((ndp,)),
            dma((nt // 2,)),
            dma((nt,)),
            dma((nt // 4, 2)),
            dma((cb, 7)),
            dma((cb, ndp)),
            dma((cb, 7)),
            dma((cb, ndp)),
            dma((2, nt // 2)),
            dma((2, nt // 2)),
            dma((2, nt // 2)),
            dma((2, nt // 2)),
            dma((ndp,)),
            dma((ndp,)),
        ],
        compiler_params=pltpu.CompilerParams(
            collective_id=0, has_side_effects=True, vmem_limit_bytes=64 * 1024 * 1024
        ),
    )(tokens, grad_out, slot, kept, gate_blocks, up_blocks, down_blocks)
    return pl.pallas_call(
        functools.partial(hand_out, 5),
        out_shape=(own_rows, own_rows, grad, grad, grad),
        in_specs=[hb] * 5,
        out_specs=[hb] * 5,
        scratch_shapes=[dma((5,))],
    )(*results)


def solution(mesh):
    rows = P(("dp", "tensor"), None)
    blocks = P("tensor", None, None)
    grads = P("tensor", "dp", None)
    return jax.shard_map(
        on_device,
        mesh=mesh,
        in_specs=(rows, rows, P(), blocks, blocks, blocks),
        out_specs=(rows, rows, grads, grads, grads),
        check_vma=False,
    )
```

```python
import functools

import jax
import jax.numpy as jnp
from jax import lax
from jax.experimental import pallas as pl
from jax.experimental.pallas import tpu as pltpu
from jax.sharding import PartitionSpec as P

MESH = pl.DeviceIdType.MESH
BF = jnp.bfloat16
F32 = jnp.float32


def nt_dot(a, b):
    return lax.dot_general(a, b, (((1,), (1,)), ((), ())), preferred_element_type=F32)


def tn_dot(a, b):
    return lax.dot_general(a, b, (((0,), (0,)), ((), ())), preferred_element_type=F32)


def swap_matrix(outer, inner):
    n = outer * inner
    o = lax.broadcasted_iota(jnp.int32, (n, n), 0)
    i = lax.broadcasted_iota(jnp.int32, (n, n), 1)
    hit = (o // outer == i % inner) & (o % outer == i // inner)
    return jnp.where(hit, 1.0, 0.0).astype(BF)


def move(a, b):
    return jnp.dot(a, b, preferred_element_type=F32).astype(BF)


def kernel(
    dims,
    tok_ref, go_ref, slot_ref, kept_ref, gate_hbm, up_hbm, down_hbm,
    mixed_ref, gtok_ref, ggate_ref, gup_ref, gdown_ref,
    stage0, stage1, wgu, wd, own16, chunks, rows, gus, acth, actg, hid, ggu, sibx, recv, fin,
    qsend, qrecv, craw, cols, tokt, gblk, ublk, dblk, dsend, drecv, perm,
    load_sem, ag_send, ag_recv, fw_send, q_send, q_recv, cg_send, cg_recv, cf_send,
    h_send, h_recv, g_send, g_recv, sib_send, sib_recv, rs_send, rs_recv, dn_send, dn_recv,
):
    ndp, nt, m, nh, rb, cb, cap = dims
    group = m * nt
    width = nh * 2048
    ds = width // ndp
    nj = ds // 128
    nchip = nt // 2
    nz = nchip // 2
    rpd = rb // ndp
    cm = m * 2 * nj // 16
    total = ndp * group
    along_y = min(1, cb)
    d = lax.axis_index("dp")
    s = lax.axis_index("tensor")
    y, x = d // 2, d % 2
    chip, core = s // 2, s % 2
    z, xh = chip // 2, chip % 2
    ny = ndp // 2

    def rdma(src, dst, ssem, rsem, dev):
        return pltpu.make_async_remote_copy(
            src_ref=src, dst_ref=dst, send_sem=ssem, recv_sem=rsem,
            device_id=dev, device_id_type=MESH,
        )

    sib = chip * 2 + (1 - core)
    xp = y * 2 + (1 - x)
    yp = lax.rem(y + 1, ny) * 2 + x
    ym = lax.rem(y + ny - 1, ny) * 2 + x
    yp_o = lax.rem(y + 1, ny) * 2 + (1 - x)
    ym_o = lax.rem(y + ny - 1, ny) * 2 + (1 - x)
    y2 = lax.rem(y + 2, ny) * 2 + x
    y2_o = lax.rem(y + 2, ny) * 2 + (1 - x)

    def chip_ahead(k):
        return lax.rem(chip + k, nchip)

    def chip_behind(k):
        return lax.rem(chip + nchip - k, nchip)

    load_g = pltpu.make_async_copy(gate_hbm, stage0.at[pl.ds(0, cap)], load_sem.at[0])
    load_u = pltpu.make_async_copy(up_hbm, stage1.at[pl.ds(0, cap)], load_sem.at[1])
    load_d = pltpu.make_async_copy(down_hbm, stage0.at[pl.ds(0, cap)], load_sem.at[2])
    barrier = pltpu.get_barrier_semaphore()
    for k in range(1, nt):
        pl.semaphore_signal(barrier, inc=1, device_id=(d, lax.rem(s + k, nt)), device_id_type=MESH)
    for k in range(1, ndp):
        pl.semaphore_signal(barrier, inc=1, device_id=(lax.rem(d + k, ndp), s), device_id_type=MESH)
    load_g.start()
    load_u.start()
    stage0[cap] = jnp.zeros((128, 128), BF)
    stage1[cap] = jnp.zeros((128, 128), BF)
    own16[...] = jnp.zeros_like(own16)
    fin[...] = jnp.zeros_like(fin)
    own16[0, 0:m, :] = tok_ref[...]
    own16[1, 0:m, :] = go_ref[...]
    perm[...] = swap_matrix(16, 16)

    for a in range(2):
        mat = jnp.concatenate(
            [
                jnp.concatenate(
                    [own16[a, :, (h * 16 + j) * 128:(h * 16 + j + 1) * 128] for j in range(16)], axis=0
                )
                for h in range(nh)
            ],
            axis=1,
        )
        out = move(perm[...], mat)
        for h in range(nh):
            chunks[a, pl.ds(s * m, m), h] = out[:, h * 128:(h + 1) * 128].reshape(16, 16, 128)[:m]
    pl.semaphore_wait(barrier, nt - 1 + ndp - 1)

    def chunk(a, src):
        return chunks.at[a, pl.ds(src * m, m)]

    def ag_copy(a, k):
        dst = chip_ahead(k) * 2 + core
        return rdma(chunk(a, s), chunk(a, s), ag_send.at[a, k], ag_recv.at[a, s], (d, dst))

    def fw_copy(a, k):
        src = chip_behind(k) * 2 + core
        return rdma(chunk(a, src), chunk(a, src), fw_send.at[a, k], ag_recv.at[a, src], (d, sib))

    def ag_arrived(a, src):
        rdma(chunk(a, src), chunk(a, src), ag_send.at[a, 0], ag_recv.at[a, src], (d, sib)).wait_recv()

    def send_own(a):
        for k in range(1, nchip):
            ag_copy(a, k).start()
        fw_copy(a, 0).start()

    send_own(0)

    def lay_inward(stage, lo):
        @pl.loop(0, rb)
        def _(r):
            for c in range(cb):
                wgu[c, pl.ds(pl.multiple_of(r * 128, 128), 128), lo:lo + 128] = stage[slot_ref[r * cb + c]]

    load_g.wait()
    lay_inward(stage0, 0)
    load_d.start()
    load_u.wait()
    send_own(1)
    lay_inward(stage1, 128)

    @pl.loop(0, ndp // 2)
    def _(pair):
        stack = jnp.concatenate(
            [own16[0, :, q * 1024:(q + 1) * 1024] for q in range(width // 1024)], axis=0
        )
        i = lax.broadcasted_iota(jnp.int32, (1024, 256), 0)
        o = lax.broadcasted_iota(jnp.int32, (1024, 256), 1) + pair * 256
        hit = (i // 128 == (o // 16) % 8) & ((i // 16) % 8 == o // 128) & (i % 16 == o % 16)
        toks = move(stack, jnp.where(hit, 1.0, 0.0).astype(BF))
        halves = []
        for w in range(2):
            base = pl.multiple_of((pair * 2 + w) * ds, 128)
            gos = jnp.concatenate(
                [own16[1, :, pl.ds(pl.multiple_of(base + j * 128, 128), 128)] for j in range(nj)], axis=0
            )
            halves.append(jnp.concatenate([toks[:, w * 128:(w + 1) * 128], gos], axis=0))
        out = move(swap_matrix(2 * nj, 16), jnp.concatenate(halves, axis=1))
        for w in range(2):
            qsend[pair * 2 + w] = out[0:cm * 16, w * 128:(w + 1) * 128].reshape(cm, 16, 128)

    def q_copy(k):
        dst = lax.rem(d + k, ndp)
        return rdma(qsend.at[dst], qrecv.at[d], q_send.at[k], q_recv.at[d], (dst, s))

    for k in range(1, ndp):
        q_copy(k).start()
    qrecv[d] = qsend[d]

    def forward(a):
        for k in range(1, nchip):
            ag_arrived(a, chip_behind(k) * 2 + core)
            fw_copy(a, k).start()

    def to_rows(a):
        @pl.loop(0, group // 16)
        def _(tb):
            t0 = pl.multiple_of(tb * 16, 16)
            mat = jnp.concatenate(
                [chunks[a, pl.ds(t0, 16), h].reshape(256, 128) for h in range(nh)], axis=1
            )
            out = move(perm[...], mat)
            for h in range(nh):
                for j in range(16):
                    lo = (h * 16 + j) * 128
                    rows[a, pl.ds(t0, 16), lo:lo + 128] = out[j * 16:(j + 1) * 16, h * 128:(h + 1) * 128]

    load_d.wait()

    @pl.loop(0, rb)
    def _(r):
        for c in range(cb):
            wd[c * 128:(c + 1) * 128, pl.ds(pl.multiple_of(r * 128, 128), 128)] = stage0[slot_ref[r * cb + c]]

    forward(0)
    for k in range(nchip):
        ag_arrived(0, chip_behind(k) * 2 + (1 - core))
    to_rows(0)

    def h_copy(c, g, n, dst):
        return rdma(acth.at[c, g], acth.at[c, g], h_send.at[c, n], h_recv.at[c, g], (dst, s))

    def h_half(c, g, part, n, dst):
        piece = acth.at[c, g, pl.ds(part * (group // 2), group // 2)]
        return rdma(piece, piece, h_send.at[c, n], h_recv.at[c, g], (dst, s))

    def g_copy(c, g, n, dst):
        return rdma(actg.at[c, g], actg.at[c, g], g_send.at[c, n], g_recv.at[c, g], (dst, s))

    def g_half(c, g, part, n, dst):
        piece = actg.at[c, g, pl.ds(part * (group // 2), group // 2)]
        return rdma(piece, piece, g_send.at[c, n], g_recv.at[c, g], (dst, s))

    @pl.loop(0, cb)
    def _(c):
        gu = jnp.dot(rows[0], wgu[c], preferred_element_type=F32)
        gus[c] = gu
        gate, up = gu[:, :128], gu[:, 128:]
        hidden = (gate * jax.nn.sigmoid(gate) * up).astype(BF)
        acth[c, d] = hidden
        h_copy(c, d, 0, xp).start()
        h_copy(c, d, 1, yp).start()
        h_copy(c, d, 2, ym).start()
        hid[:, pl.ds(pl.multiple_of(c * 128, 128), 128)] = hidden

    forward(1)
    for k in range(nchip):
        ag_arrived(1, chip_behind(k) * 2 + (1 - core))

    for k in range(1, ndp):
        src = lax.rem(d + k, ndp)
        rdma(qrecv.at[src], qrecv.at[src], q_send.at[0], q_recv.at[src], (d, sib)).wait_recv()

    def craw_of(src):
        return craw.at[:, pl.ds(src * cm, cm)]

    def at(kz, other, cr):
        along = 1 - xh if other else xh
        return (lax.rem(z + kz, nz) * 2 + along) * 2 + cr

    def cg_copy(n, dst):
        return rdma(qrecv, craw_of(s), cg_send.at[n], cg_recv.at[s], (d, dst))

    def cz_copy(k):
        src = at(0, True, core)
        return rdma(craw_of(src), craw_of(src), cg_send.at[nz + k], cg_recv.at[src], (d, at(k, False, core)))

    def cf_copy(k, other):
        src = at(k, other, core)
        return rdma(craw_of(src), craw_of(src), cf_send.at[k, other], cg_recv.at[src], (d, sib))

    def cg_arrived(src):
        rdma(craw_of(src), craw_of(src), cg_send.at[0], cg_recv.at[src], (d, sib)).wait_recv()

    cg_copy(0, sib).start()
    cg_copy(nz, at(0, True, core)).start()
    for k in range(1, nz):
        cg_copy(k, at(k, False, core)).start()
    for g in range(ndp):
        craw[g, pl.ds(s * cm, cm)] = qrecv[g]

    to_rows(1)

    @pl.loop(0, cb)
    def _(c):
        gh = nt_dot(rows[1], wd[pl.ds(pl.multiple_of(c * 128, 128), 128), :])
        gu = gus[c]
        gate, up = gu[:, :128], gu[:, 128:]
        sig = jax.nn.sigmoid(gate)
        gga = (gh * up * sig * (1.0 + gate * (1.0 - sig))).astype(BF)
        gua = (gh * (gate * sig)).astype(BF)
        actg[c, d, :, 0:128] = gga
        actg[c, d, :, 128:256] = gua
        g_copy(c, d, 0, xp).start()
        g_copy(c, d, 1, yp).start()
        g_copy(c, d, 2, ym).start()
        ggu[:, pl.ds(pl.multiple_of(c * 256, 128), 128)] = gga
        ggu[:, pl.ds(pl.multiple_of(c * 256 + 128, 128), 128)] = gua

    for a in range(2):
        for k in range(1, nchip):
            ag_copy(a, k).wait_send()
        for k in range(nchip):
            fw_copy(a, k).wait_send()
    step = min(512, width)

    def to_chunks(a):
        @pl.loop(0, group // 16)
        def _(tb):
            t0 = pl.multiple_of(tb * 16, 16)
            mat = jnp.concatenate(
                [
                    jnp.concatenate(
                        [
                            rows[a, pl.ds(t0, 16), (h * 16 + j) * 128:(h * 16 + j + 1) * 128]
                            for j in range(16)
                        ],
                        axis=0,
                    )
                    for h in range(nh)
                ],
                axis=1,
            )
            out = move(perm[...], mat)
            for h in range(nh):
                chunks[a, pl.ds(t0, 16), h] = out[:, h * 128:(h + 1) * 128].reshape(16, 16, 128)

    def sib_copy(a, q):
        return rdma(chunk(a, q * 2 + (1 - core)), sibx.at[a, q], sib_send.at[a, q], sib_recv.at[a, q], (d, sib))

    @pl.loop(along_y, cb)
    def _(c):
        h_copy(c, xp, 0, xp).wait_recv()
        h_copy(c, xp, 4, ym).start()
        h_copy(c, xp, 3, yp).start()

    cg_arrived(at(0, True, core))
    for k in range(1, nz):
        cz_copy(k).start()
    cf_copy(0, 1).start()

    @pl.loop(0, width // step)
    def _(n):
        lo = pl.multiple_of(n * step, step)
        rows[0, :, pl.ds(lo, step)] = jnp.dot(
            hid[...], wd[:, pl.ds(lo, step)], preferred_element_type=F32
        ).astype(BF)

    to_chunks(0)
    for q in range(nchip):
        sib_copy(0, q).start()

    @pl.loop(0, along_y)
    def _(c):
        h_copy(c, ym, 0, xp).wait_recv()
        h_half(c, ym, 0, 5, yp).start()
        h_copy(c, ym, 3, xp).start()
        h_copy(c, yp, 0, xp).wait_recv()
        h_half(c, yp, 1, 6, ym).start()
        h_copy(c, yp, 4, xp).start()

    @pl.loop(along_y, cb)
    def _(c):
        h_copy(c, ym, 0, xp).wait_recv()
        h_copy(c, ym, 5, yp).start()

    @pl.loop(0, width // step)
    def _(n):
        lo = pl.multiple_of(n * step, step)
        wide = jnp.concatenate([wgu[c, pl.ds(lo, step), :] for c in range(cb)], axis=1)
        rows[1, :, pl.ds(lo, step)] = nt_dot(ggu[...], wide).astype(BF)

    @pl.loop(along_y, cb)
    def _(c):
        g_copy(c, xp, 0, xp).wait_recv()
        g_copy(c, xp, 4, ym).start()
        g_copy(c, xp, 3, yp).start()

    to_chunks(1)
    for q in range(nchip):
        sib_copy(1, q).start()

    @pl.loop(0, along_y)
    def _(c):
        h_copy(c, y2, 0, xp).wait_recv()
        h_copy(c, y2, 7, xp).start()

    @pl.loop(along_y, cb)
    def _(c):
        h_copy(c, yp_o, 0, xp).wait_recv()
        h_copy(c, yp_o, 6, ym).start()

    def rs_copy(a, k):
        q = chip_ahead(k)
        return rdma(
            chunk(a, q * 2 + core), recv.at[a, chip], rs_send.at[a, k], rs_recv.at[a, chip], (d, q * 2 + core)
        )

    for a in range(2):
        for q in range(nchip):
            sib_copy(a, q).wait_recv()
        for k in range(nchip):
            q = chip_ahead(k)
            mine = pl.ds((q * 2 + core) * m, m)
            both = (chunks[a, mine].astype(F32) + sibx[a, q].astype(F32)).astype(BF)
            if k == 0:
                recv[a, chip] = both
            else:
                chunks[a, mine] = both
                rs_copy(a, k).start()

    @pl.loop(0, along_y)
    def _(c):
        g_copy(c, ym, 0, xp).wait_recv()
        g_half(c, ym, 0, 5, yp).start()
        g_copy(c, ym, 3, xp).start()
        g_copy(c, yp, 0, xp).wait_recv()
        g_half(c, yp, 1, 6, ym).start()
        g_copy(c, yp, 4, xp).start()

    @pl.loop(along_y, cb)
    def _(c):
        g_copy(c, ym, 0, xp).wait_recv()
        g_copy(c, ym, 5, yp).start()

    for k in range(1, nz):
        for other in range(2):
            cg_arrived(at(k, other, core))
            cf_copy(k, other).start()
    for k in range(nz):
        for other in range(2):
            cg_arrived(at(k, other, 1 - core))

    @pl.loop(0, ndp // 2)
    def _(gp):
        for tb in range(group // 32):
            per = 32 * 2 * nj // 16
            mat = jnp.concatenate(
                [craw[gp * 2 + w, tb * per:(tb + 1) * per].reshape(per * 16, 128) for w in range(2)], axis=1
            )
            out = move(swap_matrix(32, 2 * nj), mat)
            for w in range(2):
                for a in range(2):
                    for j in range(nj):
                        lo = (a * nj + j) * 32
                        cols[a, gp * 2 + w, tb * 32:(tb + 1) * 32, j * 128:(j + 1) * 128] = (
                            out[lo:lo + 32, w * 128:(w + 1) * 128]
                        )

    tall = cols[0].reshape(total, ds)
    for q in range(total // 128):
        tokt[:, q * 128:(q + 1) * 128] = tall[q * 128:(q + 1) * 128].T

    def dn_copy(c, k):
        dst = lax.rem(d + k, ndp)
        return rdma(dsend.at[dst, c], drecv.at[d, c], dn_send.at[k], dn_recv.at[d], (dst, s))

    def grad_down(c):
        down = tn_dot(acth[c].reshape(total, 128), cols[1].reshape(total, ds)).astype(BF)
        for o in range(ndp):
            dsend[o, c] = down[o * 16:(o + 1) * 16]
        for k in range(1, ndp):
            dn_copy(c, k).start()
        drecv[d, c] = dsend[d, c]

    @pl.loop(0, along_y)
    def _(c):
        for g in (xp, ym_o, yp_o, y2_o):
            h_copy(c, g, 0, xp).wait_recv()
        grad_down(c)

    @pl.loop(along_y, cb)
    def _(c):
        for g in (ym_o, yp, y2, y2_o):
            h_copy(c, g, 0, xp).wait_recv()
        grad_down(c)

    @pl.loop(0, along_y)
    def _(c):
        g_copy(c, y2, 0, xp).wait_recv()
        g_copy(c, y2, 7, xp).start()

    @pl.loop(along_y, cb)
    def _(c):
        g_copy(c, yp_o, 0, xp).wait_recv()
        g_copy(c, yp_o, 6, ym).start()

    for a, out_ref in ((0, mixed_ref), (1, gtok_ref)):
        for k in range(1, nchip):
            q = chip_ahead(k)
            rdma(recv.at[a, q], recv.at[a, q], rs_send.at[a, 0], rs_recv.at[a, q], (d, sib)).wait_recv()
        fin[0:m] = jnp.sum(recv[a].astype(F32), axis=0).astype(BF)
        mat = jnp.concatenate([fin[:, h].reshape(256, 128) for h in range(nh)], axis=1)
        out = move(perm[...], mat)
        for h in range(nh):
            for j in range(16):
                lo = (h * 16 + j) * 128
                out_ref[:, lo:lo + 128] = out[j * 16:j * 16 + m, h * 128:(h + 1) * 128]

    def grad_inward(c):
        both = jnp.dot(tokt[...], actg[c].reshape(total, 256), preferred_element_type=F32).astype(BF)
        for r in range(rb):
            gblk[r * cb + c] = both[r * 16:(r + 1) * 16, :128]
            ublk[r * cb + c] = both[r * 16:(r + 1) * 16, 128:]

    @pl.loop(0, along_y)
    def _(c):
        for g in (xp, ym_o, yp_o, y2_o):
            g_copy(c, g, 0, xp).wait_recv()
        grad_inward(c)

    @pl.loop(along_y, cb)
    def _(c):
        for g in (ym_o, yp, y2, y2_o):
            g_copy(c, g, 0, xp).wait_recv()
        grad_inward(c)

    zero = jnp.zeros((16, 128), BF)
    gblk[rb * cb] = zero
    ublk[rb * cb] = zero
    dblk[rb * cb] = zero

    for k in range(1, ndp):
        src = lax.rem(d + k, ndp)
        rdma(drecv.at[src], drecv.at[src], dn_send.at[0], dn_recv.at[src], (d, sib)).wait_recv()
    for r in range(rb):
        for c in range(cb):
            lo = (r % rpd) * 128
            dblk[r * cb + c] = drecv[r // rpd, c, :, lo:lo + 128]

    @pl.loop(0, cap)
    def _(k):
        ggate_ref[k] = gblk[kept_ref[k]]
        gup_ref[k] = ublk[kept_ref[k]]
        gdown_ref[k] = dblk[kept_ref[k]]

    for k in range(1, ndp):
        q_copy(k).wait_send()
        rdma(dsend.at[lax.rem(d + k, ndp)], drecv.at[d], dn_send.at[k], dn_recv.at[d], (d, sib)).wait_send()
    cg_copy(0, sib).wait_send()
    cg_copy(nz, sib).wait_send()
    cf_copy(0, 1).wait_send()
    for k in range(1, nz):
        cg_copy(k, sib).wait_send()
        cz_copy(k).wait_send()
        for other in range(2):
            cf_copy(k, other).wait_send()
    for a in range(2):
        for q in range(nchip):
            sib_copy(a, q).wait_send()
        for k in range(1, nchip):
            rs_copy(a, k).wait_send()

    @pl.loop(0, along_y)
    def _(c):
        for n, g in ((0, d), (1, d), (2, d), (3, ym), (4, yp), (7, y2)):
            h_copy(c, g, n, xp).wait_send()
            g_copy(c, g, n, xp).wait_send()
        for n, g in ((5, ym), (6, yp)):
            h_half(c, g, 0, n, xp).wait_send()
            g_half(c, g, 0, n, xp).wait_send()

    @pl.loop(along_y, cb)
    def _(c):
        for n, g in enumerate((d, d, d, xp, xp, ym, yp_o)):
            h_copy(c, g, n, xp).wait_send()
            g_copy(c, g, n, xp).wait_send()


def hand_out(n, *refs):
    given, results, held, sems = refs[:n], refs[n:2 * n], refs[2 * n:3 * n], refs[3 * n]
    loads = [pltpu.make_async_copy(given[i], held[i], sems.at[0, i]) for i in range(n)]
    stores = [pltpu.make_async_copy(held[i], results[i], sems.at[1, i]) for i in range(n)]
    for load in loads:
        load.start()
    for load, store in zip(loads, stores):
        load.wait()
        store.start()
    for store in stores:
        store.wait()


def on_device(tokens, grad_out, block_mask, gate_blocks, up_blocks, down_blocks):
    nt = lax.axis_size("tensor")
    ndp = lax.axis_size("dp")
    shard = lax.axis_index("tensor")
    rb = block_mask.shape[0]
    cb = block_mask.shape[1] // nt
    cap = gate_blocks.shape[0]
    m, width = tokens.shape
    nh = width // 2048
    group = m * nt
    ds = width // ndp
    nb = rb * cb
    cm = m * 2 * (ds // 128) // 16
    flags = lax.dynamic_slice_in_dim(block_mask, shard * cb, cb, 1).reshape(-1)
    pos = jnp.arange(nb, dtype=jnp.int32)
    upto = jnp.sum(jnp.where(pos[None, :] <= pos[:, None], flags[None, :], 0), axis=1)
    slot = jnp.where(flags > 0, upto - 1, cap)
    kept = jnp.sum((upto[None, :] <= jnp.arange(cap, dtype=jnp.int32)[:, None]).astype(jnp.int32), axis=1)

    vm = pl.BlockSpec(memory_space=pltpu.VMEM)
    sm = pl.BlockSpec(memory_space=pltpu.SMEM)
    hb = pl.BlockSpec(memory_space=pl.ANY)
    dma = pltpu.SemaphoreType.DMA
    own_rows = jax.ShapeDtypeStruct((m, width), BF)
    grad = jax.ShapeDtypeStruct((cap, 16, 128), BF)
    results = pl.pallas_call(
        functools.partial(kernel, (ndp, nt, m, nh, rb, cb, cap)),
        out_shape=(own_rows, own_rows, grad, grad, grad),
        in_specs=[vm, vm, sm, sm, hb, hb, hb],
        out_specs=[vm] * 5,
        scratch_shapes=[
            pltpu.VMEM((cap + 1, 128, 128), BF),
            pltpu.VMEM((cap + 1, 128, 128), BF),
            pltpu.VMEM((cb, width, 256), BF),
            pltpu.VMEM((cb * 128, width), BF),
            pltpu.VMEM((2, 16, width), BF),
            pltpu.VMEM((2, group, nh, 16, 128), BF),
            pltpu.VMEM((2, group, width), BF),
            pltpu.VMEM((cb, group, 256), F32),
            pltpu.VMEM((cb, ndp, group, 128), BF),
            pltpu.VMEM((cb, ndp, group, 256), BF),
            pltpu.VMEM((group, cb * 128), BF),
            pltpu.VMEM((group, cb * 256), BF),
            pltpu.VMEM((2, nt // 2, m, nh, 16, 128), BF),
            pltpu.VMEM((2, nt // 2, m, nh, 16, 128), BF),
            pltpu.VMEM((16, nh, 16, 128), BF),
            pltpu.VMEM((ndp, cm, 16, 128), BF),
            pltpu.VMEM((ndp, cm, 16, 128), BF),
            pltpu.VMEM((ndp, nt * cm, 16, 128), BF),
            pltpu.VMEM((2, ndp, group, ds), BF),
            pltpu.VMEM((ds, ndp * group), BF),
            pltpu.VMEM((nb + 1, 16, 128), BF),
            pltpu.VMEM((nb + 1, 16, 128), BF),
            pltpu.VMEM((nb + 1, 16, 128), BF),
            pltpu.VMEM((ndp, cb, 16, ds), BF),
            pltpu.VMEM((ndp, cb, 16, ds), BF),
            pltpu.VMEM((256, 256), BF),
            dma((3,)),
            dma((2, nt // 2)),
            dma((2, nt)),
            dma((2, nt // 2)),
            dma((ndp,)),
            dma((ndp,)),
            dma((nt // 2,)),
            dma((nt,)),
            dma((nt // 4, 2)),
            dma((cb, 8)),
            dma((cb, ndp)),
            dma((cb, 8)),
            dma((cb, ndp)),
            dma((2, nt // 2)),
            dma((2, nt // 2)),
            dma((2, nt // 2)),
            dma((2, nt // 2)),
            dma((ndp,)),
            dma((ndp,)),
        ],
        compiler_params=pltpu.CompilerParams(
            collective_id=0, has_side_effects=True, vmem_limit_bytes=64 * 1024 * 1024
        ),
    )(tokens, grad_out, slot, kept, gate_blocks, up_blocks, down_blocks)
    return pl.pallas_call(
        functools.partial(hand_out, 5),
        out_shape=(own_rows, own_rows, grad, grad, grad),
        in_specs=[hb] * 5,
        out_specs=[hb] * 5,
        scratch_shapes=[pltpu.VMEM(out.shape, BF) for out in (own_rows, own_rows, grad, grad, grad)]
        + [dma((2, 5))],
    )(*results)


def solution(mesh):
    rows = P(("dp", "tensor"), None)
    blocks = P("tensor", None, None)
    grads = P("tensor", "dp", None)
    return jax.shard_map(
        on_device,
        mesh=mesh,
        in_specs=(rows, rows, P(), blocks, blocks, blocks),
        out_specs=(rows, rows, grads, grads, grads),
        check_vma=False,
    )
```

```python
import functools

import jax
import jax.numpy as jnp
from jax import lax
from jax.experimental import pallas as pl
from jax.experimental.pallas import tpu as pltpu
from jax.sharding import PartitionSpec as P

MESH = pl.DeviceIdType.MESH
BF = jnp.bfloat16
F32 = jnp.float32


def nt_dot(a, b):
    return lax.dot_general(a, b, (((1,), (1,)), ((), ())), preferred_element_type=F32)


def tn_dot(a, b):
    return lax.dot_general(a, b, (((0,), (0,)), ((), ())), preferred_element_type=F32)


def swap_matrix(outer, inner):
    n = outer * inner
    o = lax.broadcasted_iota(jnp.int32, (n, n), 0)
    i = lax.broadcasted_iota(jnp.int32, (n, n), 1)
    hit = (o // outer == i % inner) & (o % outer == i // inner)
    return jnp.where(hit, 1.0, 0.0).astype(BF)


def move(a, b):
    return jnp.dot(a, b, preferred_element_type=F32).astype(BF)


def kernel(
    dims,
    tok_ref, go_ref, slot_ref, kept_ref, gate_hbm, up_hbm, down_hbm,
    mixed_ref, gtok_ref, ggate_ref, gup_ref, gdown_ref,
    stage0, stage1, wgu, wd, own16, chunks, rows, gus, acth, actg, hid, ggu, sibx, recv, fin,
    qsend, qrecv, craw, cols, tokt, gblk, ublk, dblk, dsend, drecv, perm,
    load_sem, ag_send, ag_recv, fw_send, q_send, q_recv, cg_send, cg_recv, cf_send,
    h_send, h_recv, g_send, g_recv, sib_send, sib_recv, rs_send, rs_recv, dn_send, dn_recv,
):
    ndp, nt, m, nh, rb, cb, cap = dims
    group = m * nt
    width = nh * 2048
    ds = width // ndp
    nj = ds // 128
    nchip = nt // 2
    nz = nchip // 2
    rpd = rb // ndp
    cm = m * 2 * nj // 16
    total = ndp * group
    along_h, along_g = min(2, cb), min(1, cb)
    d = lax.axis_index("dp")
    s = lax.axis_index("tensor")
    y, x = d // 2, d % 2
    chip, core = s // 2, s % 2
    z, xh = chip // 2, chip % 2
    ny = ndp // 2

    def rdma(src, dst, ssem, rsem, dev):
        return pltpu.make_async_remote_copy(
            src_ref=src, dst_ref=dst, send_sem=ssem, recv_sem=rsem,
            device_id=dev, device_id_type=MESH,
        )

    sib = chip * 2 + (1 - core)
    xp = y * 2 + (1 - x)
    yp = lax.rem(y + 1, ny) * 2 + x
    ym = lax.rem(y + ny - 1, ny) * 2 + x
    yp_o = lax.rem(y + 1, ny) * 2 + (1 - x)
    ym_o = lax.rem(y + ny - 1, ny) * 2 + (1 - x)
    y2 = lax.rem(y + 2, ny) * 2 + x
    y2_o = lax.rem(y + 2, ny) * 2 + (1 - x)

    def chip_ahead(k):
        return lax.rem(chip + k, nchip)

    def chip_behind(k):
        return lax.rem(chip + nchip - k, nchip)

    load_g = pltpu.make_async_copy(gate_hbm, stage0.at[pl.ds(0, cap)], load_sem.at[0])
    load_u = pltpu.make_async_copy(up_hbm, stage1.at[pl.ds(0, cap)], load_sem.at[1])
    load_d = pltpu.make_async_copy(down_hbm, stage0.at[pl.ds(0, cap)], load_sem.at[2])
    barrier = pltpu.get_barrier_semaphore()
    for k in range(1, nt):
        pl.semaphore_signal(barrier, inc=1, device_id=(d, lax.rem(s + k, nt)), device_id_type=MESH)
    for k in range(1, ndp):
        pl.semaphore_signal(barrier, inc=1, device_id=(lax.rem(d + k, ndp), s), device_id_type=MESH)
    load_g.start()
    load_u.start()
    stage0[cap] = jnp.zeros((128, 128), BF)
    stage1[cap] = jnp.zeros((128, 128), BF)
    own16[...] = jnp.zeros_like(own16)
    fin[...] = jnp.zeros_like(fin)
    own16[0, 0:m, :] = tok_ref[...]
    own16[1, 0:m, :] = go_ref[...]
    perm[...] = swap_matrix(16, 16)

    for a in range(2):
        mat = jnp.concatenate(
            [
                jnp.concatenate(
                    [own16[a, :, (h * 16 + j) * 128:(h * 16 + j + 1) * 128] for j in range(16)], axis=0
                )
                for h in range(nh)
            ],
            axis=1,
        )
        out = move(perm[...], mat)
        for h in range(nh):
            chunks[a, pl.ds(s * m, m), h] = out[:, h * 128:(h + 1) * 128].reshape(16, 16, 128)[:m]
    pl.semaphore_wait(barrier, nt - 1 + ndp - 1)

    def chunk(a, src):
        return chunks.at[a, pl.ds(src * m, m)]

    def ag_copy(a, k):
        dst = chip_ahead(k) * 2 + core
        return rdma(chunk(a, s), chunk(a, s), ag_send.at[a, k], ag_recv.at[a, s], (d, dst))

    def fw_copy(a, k):
        src = chip_behind(k) * 2 + core
        return rdma(chunk(a, src), chunk(a, src), fw_send.at[a, k], ag_recv.at[a, src], (d, sib))

    def ag_arrived(a, src):
        rdma(chunk(a, src), chunk(a, src), ag_send.at[a, 0], ag_recv.at[a, src], (d, sib)).wait_recv()

    def send_own(a):
        for k in range(1, nchip):
            ag_copy(a, k).start()
        fw_copy(a, 0).start()

    send_own(0)

    def lay_inward(stage, lo):
        @pl.loop(0, rb)
        def _(r):
            for c in range(cb):
                wgu[c, pl.ds(pl.multiple_of(r * 128, 128), 128), lo:lo + 128] = stage[slot_ref[r * cb + c]]

    load_g.wait()
    lay_inward(stage0, 0)
    load_d.start()
    load_u.wait()
    send_own(1)
    lay_inward(stage1, 128)

    @pl.loop(0, ndp // 2)
    def _(pair):
        stack = jnp.concatenate(
            [own16[0, :, q * 1024:(q + 1) * 1024] for q in range(width // 1024)], axis=0
        )
        i = lax.broadcasted_iota(jnp.int32, (1024, 256), 0)
        o = lax.broadcasted_iota(jnp.int32, (1024, 256), 1) + pair * 256
        hit = (i // 128 == (o // 16) % 8) & ((i // 16) % 8 == o // 128) & (i % 16 == o % 16)
        toks = move(stack, jnp.where(hit, 1.0, 0.0).astype(BF))
        halves = []
        for w in range(2):
            base = pl.multiple_of((pair * 2 + w) * ds, 128)
            gos = jnp.concatenate(
                [own16[1, :, pl.ds(pl.multiple_of(base + j * 128, 128), 128)] for j in range(nj)], axis=0
            )
            halves.append(jnp.concatenate([toks[:, w * 128:(w + 1) * 128], gos], axis=0))
        out = move(swap_matrix(2 * nj, 16), jnp.concatenate(halves, axis=1))
        for w in range(2):
            qsend[pair * 2 + w] = out[0:cm * 16, w * 128:(w + 1) * 128].reshape(cm, 16, 128)

    def q_copy(k):
        dst = lax.rem(d + k, ndp)
        return rdma(qsend.at[dst], qrecv.at[d], q_send.at[k], q_recv.at[d], (dst, s))

    for k in range(1, ndp):
        q_copy(k).start()
    qrecv[d] = qsend[d]

    def forward(a):
        for k in range(1, nchip):
            ag_arrived(a, chip_behind(k) * 2 + core)
            fw_copy(a, k).start()

    def to_rows(a):
        @pl.loop(0, group // 16)
        def _(tb):
            t0 = pl.multiple_of(tb * 16, 16)
            mat = jnp.concatenate(
                [chunks[a, pl.ds(t0, 16), h].reshape(256, 128) for h in range(nh)], axis=1
            )
            out = move(perm[...], mat)
            for h in range(nh):
                for j in range(16):
                    lo = (h * 16 + j) * 128
                    rows[a, pl.ds(t0, 16), lo:lo + 128] = out[j * 16:(j + 1) * 16, h * 128:(h + 1) * 128]

    load_d.wait()

    @pl.loop(0, rb)
    def _(r):
        for c in range(cb):
            wd[c * 128:(c + 1) * 128, pl.ds(pl.multiple_of(r * 128, 128), 128)] = stage0[slot_ref[r * cb + c]]

    forward(0)
    for k in range(nchip):
        ag_arrived(0, chip_behind(k) * 2 + (1 - core))
    to_rows(0)

    def h_copy(c, g, n, dst):
        return rdma(acth.at[c, g], acth.at[c, g], h_send.at[c, n], h_recv.at[c, g], (dst, s))

    def h_half(c, g, part, n, dst):
        piece = acth.at[c, g, pl.ds(part * (group // 2), group // 2)]
        return rdma(piece, piece, h_send.at[c, n], h_recv.at[c, g], (dst, s))

    def g_copy(c, g, n, dst):
        return rdma(actg.at[c, g], actg.at[c, g], g_send.at[c, n], g_recv.at[c, g], (dst, s))

    def g_half(c, g, part, n, dst):
        piece = actg.at[c, g, pl.ds(part * (group // 2), group // 2)]
        return rdma(piece, piece, g_send.at[c, n], g_recv.at[c, g], (dst, s))

    @pl.loop(0, cb)
    def _(c):
        gu = jnp.dot(rows[0], wgu[c], preferred_element_type=F32)
        gus[c] = gu
        gate, up = gu[:, :128], gu[:, 128:]
        hidden = (gate * jax.nn.sigmoid(gate) * up).astype(BF)
        acth[c, d] = hidden
        h_copy(c, d, 0, xp).start()
        h_copy(c, d, 1, yp).start()
        h_copy(c, d, 2, ym).start()
        hid[:, pl.ds(pl.multiple_of(c * 128, 128), 128)] = hidden

    forward(1)
    for k in range(nchip):
        ag_arrived(1, chip_behind(k) * 2 + (1 - core))

    for k in range(1, ndp):
        src = lax.rem(d + k, ndp)
        rdma(qrecv.at[src], qrecv.at[src], q_send.at[0], q_recv.at[src], (d, sib)).wait_recv()

    def craw_of(src):
        return craw.at[:, pl.ds(src * cm, cm)]

    def at(kz, other, cr):
        along = 1 - xh if other else xh
        return (lax.rem(z + kz, nz) * 2 + along) * 2 + cr

    def cg_copy(n, dst):
        return rdma(qrecv, craw_of(s), cg_send.at[n], cg_recv.at[s], (d, dst))

    def cz_copy(k):
        src = at(0, True, core)
        return rdma(craw_of(src), craw_of(src), cg_send.at[nz + k], cg_recv.at[src], (d, at(k, False, core)))

    def cf_copy(k, other):
        src = at(k, other, core)
        return rdma(craw_of(src), craw_of(src), cf_send.at[k, other], cg_recv.at[src], (d, sib))

    def cg_arrived(src):
        rdma(craw_of(src), craw_of(src), cg_send.at[0], cg_recv.at[src], (d, sib)).wait_recv()

    cg_copy(0, sib).start()
    cg_copy(nz, at(0, True, core)).start()
    for k in range(1, nz):
        cg_copy(k, at(k, False, core)).start()
    for g in range(ndp):
        craw[g, pl.ds(s * cm, cm)] = qrecv[g]

    to_rows(1)

    @pl.loop(0, cb)
    def _(c):
        gh = nt_dot(rows[1], wd[pl.ds(pl.multiple_of(c * 128, 128), 128), :])
        gu = gus[c]
        gate, up = gu[:, :128], gu[:, 128:]
        sig = jax.nn.sigmoid(gate)
        gga = (gh * up * sig * (1.0 + gate * (1.0 - sig))).astype(BF)
        gua = (gh * (gate * sig)).astype(BF)
        actg[c, d, :, 0:128] = gga
        actg[c, d, :, 128:256] = gua
        g_copy(c, d, 0, xp).start()
        g_copy(c, d, 1, yp).start()
        g_copy(c, d, 2, ym).start()
        ggu[:, pl.ds(pl.multiple_of(c * 256, 128), 128)] = gga
        ggu[:, pl.ds(pl.multiple_of(c * 256 + 128, 128), 128)] = gua

    for a in range(2):
        for k in range(1, nchip):
            ag_copy(a, k).wait_send()
        for k in range(nchip):
            fw_copy(a, k).wait_send()
    step = min(512, width)

    def to_chunks(a):
        @pl.loop(0, group // 16)
        def _(tb):
            t0 = pl.multiple_of(tb * 16, 16)
            mat = jnp.concatenate(
                [
                    jnp.concatenate(
                        [
                            rows[a, pl.ds(t0, 16), (h * 16 + j) * 128:(h * 16 + j + 1) * 128]
                            for j in range(16)
                        ],
                        axis=0,
                    )
                    for h in range(nh)
                ],
                axis=1,
            )
            out = move(perm[...], mat)
            for h in range(nh):
                chunks[a, pl.ds(t0, 16), h] = out[:, h * 128:(h + 1) * 128].reshape(16, 16, 128)

    def sib_copy(a, q):
        return rdma(chunk(a, q * 2 + (1 - core)), sibx.at[a, q], sib_send.at[a, q], sib_recv.at[a, q], (d, sib))

    @pl.loop(along_h, cb)
    def _(c):
        h_copy(c, xp, 0, xp).wait_recv()
        h_copy(c, xp, 4, ym).start()
        h_copy(c, xp, 3, yp).start()

    cg_arrived(at(0, True, core))
    for k in range(1, nz):
        cz_copy(k).start()
    cf_copy(0, 1).start()

    @pl.loop(0, width // step)
    def _(n):
        lo = pl.multiple_of(n * step, step)
        rows[0, :, pl.ds(lo, step)] = jnp.dot(
            hid[...], wd[:, pl.ds(lo, step)], preferred_element_type=F32
        ).astype(BF)

    to_chunks(0)
    for q in range(nchip):
        sib_copy(0, q).start()

    @pl.loop(0, along_h)
    def _(c):
        h_copy(c, ym, 0, xp).wait_recv()
        h_half(c, ym, 0, 5, yp).start()
        h_copy(c, ym, 3, xp).start()
        h_copy(c, yp, 0, xp).wait_recv()
        h_half(c, yp, 1, 6, ym).start()
        h_copy(c, yp, 4, xp).start()

    @pl.loop(along_h, cb)
    def _(c):
        h_copy(c, ym, 0, xp).wait_recv()
        h_copy(c, ym, 5, yp).start()

    @pl.loop(0, width // step)
    def _(n):
        lo = pl.multiple_of(n * step, step)
        wide = jnp.concatenate([wgu[c, pl.ds(lo, step), :] for c in range(cb)], axis=1)
        rows[1, :, pl.ds(lo, step)] = nt_dot(ggu[...], wide).astype(BF)

    @pl.loop(along_g, cb)
    def _(c):
        g_copy(c, xp, 0, xp).wait_recv()
        g_copy(c, xp, 4, ym).start()
        g_copy(c, xp, 3, yp).start()

    to_chunks(1)
    for q in range(nchip):
        sib_copy(1, q).start()

    @pl.loop(0, along_h)
    def _(c):
        h_copy(c, y2, 0, xp).wait_recv()
        h_copy(c, y2, 7, xp).start()

    @pl.loop(along_h, cb)
    def _(c):
        h_copy(c, yp_o, 0, xp).wait_recv()
        h_copy(c, yp_o, 6, ym).start()

    def rs_copy(a, k):
        q = chip_ahead(k)
        return rdma(
            chunk(a, q * 2 + core), recv.at[a, chip], rs_send.at[a, k], rs_recv.at[a, chip], (d, q * 2 + core)
        )

    for a in range(2):
        for q in range(nchip):
            sib_copy(a, q).wait_recv()
        for k in range(nchip):
            q = chip_ahead(k)
            mine = pl.ds((q * 2 + core) * m, m)
            both = (chunks[a, mine].astype(F32) + sibx[a, q].astype(F32)).astype(BF)
            if k == 0:
                recv[a, chip] = both
            else:
                chunks[a, mine] = both
                rs_copy(a, k).start()

    @pl.loop(0, along_g)
    def _(c):
        g_copy(c, ym, 0, xp).wait_recv()
        g_half(c, ym, 0, 5, yp).start()
        g_copy(c, ym, 3, xp).start()
        g_copy(c, yp, 0, xp).wait_recv()
        g_half(c, yp, 1, 6, ym).start()
        g_copy(c, yp, 4, xp).start()

    @pl.loop(along_g, cb)
    def _(c):
        g_copy(c, ym, 0, xp).wait_recv()
        g_copy(c, ym, 5, yp).start()

    for k in range(1, nz):
        for other in range(2):
            cg_arrived(at(k, other, core))
            cf_copy(k, other).start()
    for k in range(nz):
        for other in range(2):
            cg_arrived(at(k, other, 1 - core))

    @pl.loop(0, ndp // 2)
    def _(gp):
        for tb in range(group // 32):
            per = 32 * 2 * nj // 16
            mat = jnp.concatenate(
                [craw[gp * 2 + w, tb * per:(tb + 1) * per].reshape(per * 16, 128) for w in range(2)], axis=1
            )
            out = move(swap_matrix(32, 2 * nj), mat)
            for w in range(2):
                for a in range(2):
                    for j in range(nj):
                        lo = (a * nj + j) * 32
                        cols[a, gp * 2 + w, tb * 32:(tb + 1) * 32, j * 128:(j + 1) * 128] = (
                            out[lo:lo + 32, w * 128:(w + 1) * 128]
                        )

    tall = cols[0].reshape(total, ds)
    for q in range(total // 128):
        tokt[:, q * 128:(q + 1) * 128] = tall[q * 128:(q + 1) * 128].T

    def dn_copy(c, k):
        dst = lax.rem(d + k, ndp)
        return rdma(dsend.at[dst, c], drecv.at[d, c], dn_send.at[k], dn_recv.at[d], (dst, s))

    def grad_down(c):
        down = tn_dot(acth[c].reshape(total, 128), cols[1].reshape(total, ds)).astype(BF)
        for o in range(ndp):
            dsend[o, c] = down[o * 16:(o + 1) * 16]
        for k in range(1, ndp):
            dn_copy(c, k).start()
        drecv[d, c] = dsend[d, c]

    @pl.loop(0, along_h)
    def _(c):
        for g in (xp, ym_o, yp_o, y2_o):
            h_copy(c, g, 0, xp).wait_recv()
        grad_down(c)

    @pl.loop(along_h, cb)
    def _(c):
        for g in (ym_o, yp, y2, y2_o):
            h_copy(c, g, 0, xp).wait_recv()
        grad_down(c)

    @pl.loop(0, along_g)
    def _(c):
        g_copy(c, y2, 0, xp).wait_recv()
        g_copy(c, y2, 7, xp).start()

    @pl.loop(along_g, cb)
    def _(c):
        g_copy(c, yp_o, 0, xp).wait_recv()
        g_copy(c, yp_o, 6, ym).start()

    for a, out_ref in ((0, mixed_ref), (1, gtok_ref)):
        for k in range(1, nchip):
            q = chip_ahead(k)
            rdma(recv.at[a, q], recv.at[a, q], rs_send.at[a, 0], rs_recv.at[a, q], (d, sib)).wait_recv()
        fin[0:m] = jnp.sum(recv[a].astype(F32), axis=0).astype(BF)
        mat = jnp.concatenate([fin[:, h].reshape(256, 128) for h in range(nh)], axis=1)
        out = move(perm[...], mat)
        for h in range(nh):
            for j in range(16):
                lo = (h * 16 + j) * 128
                out_ref[:, lo:lo + 128] = out[j * 16:j * 16 + m, h * 128:(h + 1) * 128]

    def grad_inward(c):
        both = jnp.dot(tokt[...], actg[c].reshape(total, 256), preferred_element_type=F32).astype(BF)
        for r in range(rb):
            gblk[r * cb + c] = both[r * 16:(r + 1) * 16, :128]
            ublk[r * cb + c] = both[r * 16:(r + 1) * 16, 128:]

    @pl.loop(0, along_g)
    def _(c):
        for g in (xp, ym_o, yp_o, y2_o):
            g_copy(c, g, 0, xp).wait_recv()
        grad_inward(c)

    @pl.loop(along_g, cb)
    def _(c):
        for g in (ym_o, yp, y2, y2_o):
            g_copy(c, g, 0, xp).wait_recv()
        grad_inward(c)

    zero = jnp.zeros((16, 128), BF)
    gblk[rb * cb] = zero
    ublk[rb * cb] = zero
    dblk[rb * cb] = zero

    for k in range(1, ndp):
        src = lax.rem(d + k, ndp)
        rdma(drecv.at[src], drecv.at[src], dn_send.at[0], dn_recv.at[src], (d, sib)).wait_recv()
    for r in range(rb):
        for c in range(cb):
            lo = (r % rpd) * 128
            dblk[r * cb + c] = drecv[r // rpd, c, :, lo:lo + 128]

    @pl.loop(0, cap)
    def _(k):
        ggate_ref[k] = gblk[kept_ref[k]]
        gup_ref[k] = ublk[kept_ref[k]]
        gdown_ref[k] = dblk[kept_ref[k]]

    for k in range(1, ndp):
        q_copy(k).wait_send()
        rdma(dsend.at[lax.rem(d + k, ndp)], drecv.at[d], dn_send.at[k], dn_recv.at[d], (d, sib)).wait_send()
    cg_copy(0, sib).wait_send()
    cg_copy(nz, sib).wait_send()
    cf_copy(0, 1).wait_send()
    for k in range(1, nz):
        cg_copy(k, sib).wait_send()
        cz_copy(k).wait_send()
        for other in range(2):
            cf_copy(k, other).wait_send()
    for a in range(2):
        for q in range(nchip):
            sib_copy(a, q).wait_send()
        for k in range(1, nchip):
            rs_copy(a, k).wait_send()

    @pl.loop(0, along_h)
    def _(c):
        for n, g in ((0, d), (1, d), (2, d), (3, ym), (4, yp), (7, y2)):
            h_copy(c, g, n, xp).wait_send()
        for n, g in ((5, ym), (6, yp)):
            h_half(c, g, 0, n, xp).wait_send()

    @pl.loop(along_h, cb)
    def _(c):
        for n, g in enumerate((d, d, d, xp, xp, ym, yp_o)):
            h_copy(c, g, n, xp).wait_send()

    @pl.loop(0, along_g)
    def _(c):
        for n, g in ((0, d), (1, d), (2, d), (3, ym), (4, yp), (7, y2)):
            g_copy(c, g, n, xp).wait_send()
        for n, g in ((5, ym), (6, yp)):
            g_half(c, g, 0, n, xp).wait_send()

    @pl.loop(along_g, cb)
    def _(c):
        for n, g in enumerate((d, d, d, xp, xp, ym, yp_o)):
            g_copy(c, g, n, xp).wait_send()


def hand_out(n, *refs):
    given, results, held, sems = refs[:n], refs[n:2 * n], refs[2 * n:3 * n], refs[3 * n]
    loads = [pltpu.make_async_copy(given[i], held[i], sems.at[0, i]) for i in range(n)]
    stores = [pltpu.make_async_copy(held[i], results[i], sems.at[1, i]) for i in range(n)]
    for load in loads:
        load.start()
    for load, store in zip(loads, stores):
        load.wait()
        store.start()
    for store in stores:
        store.wait()


def on_device(tokens, grad_out, block_mask, gate_blocks, up_blocks, down_blocks):
    nt = lax.axis_size("tensor")
    ndp = lax.axis_size("dp")
    shard = lax.axis_index("tensor")
    rb = block_mask.shape[0]
    cb = block_mask.shape[1] // nt
    cap = gate_blocks.shape[0]
    m, width = tokens.shape
    nh = width // 2048
    group = m * nt
    ds = width // ndp
    nb = rb * cb
    cm = m * 2 * (ds // 128) // 16
    flags = lax.dynamic_slice_in_dim(block_mask, shard * cb, cb, 1).reshape(-1)
    pos = jnp.arange(nb, dtype=jnp.int32)
    upto = jnp.sum(jnp.where(pos[None, :] <= pos[:, None], flags[None, :], 0), axis=1)
    slot = jnp.where(flags > 0, upto - 1, cap)
    kept = jnp.sum((upto[None, :] <= jnp.arange(cap, dtype=jnp.int32)[:, None]).astype(jnp.int32), axis=1)

    vm = pl.BlockSpec(memory_space=pltpu.VMEM)
    sm = pl.BlockSpec(memory_space=pltpu.SMEM)
    hb = pl.BlockSpec(memory_space=pl.ANY)
    dma = pltpu.SemaphoreType.DMA
    own_rows = jax.ShapeDtypeStruct((m, width), BF)
    grad = jax.ShapeDtypeStruct((cap, 16, 128), BF)
    results = pl.pallas_call(
        functools.partial(kernel, (ndp, nt, m, nh, rb, cb, cap)),
        out_shape=(own_rows, own_rows, grad, grad, grad),
        in_specs=[vm, vm, sm, sm, hb, hb, hb],
        out_specs=[vm] * 5,
        scratch_shapes=[
            pltpu.VMEM((cap + 1, 128, 128), BF),
            pltpu.VMEM((cap + 1, 128, 128), BF),
            pltpu.VMEM((cb, width, 256), BF),
            pltpu.VMEM((cb * 128, width), BF),
            pltpu.VMEM((2, 16, width), BF),
            pltpu.VMEM((2, group, nh, 16, 128), BF),
            pltpu.VMEM((2, group, width), BF),
            pltpu.VMEM((cb, group, 256), F32),
            pltpu.VMEM((cb, ndp, group, 128), BF),
            pltpu.VMEM((cb, ndp, group, 256), BF),
            pltpu.VMEM((group, cb * 128), BF),
            pltpu.VMEM((group, cb * 256), BF),
            pltpu.VMEM((2, nt // 2, m, nh, 16, 128), BF),
            pltpu.VMEM((2, nt // 2, m, nh, 16, 128), BF),
            pltpu.VMEM((16, nh, 16, 128), BF),
            pltpu.VMEM((ndp, cm, 16, 128), BF),
            pltpu.VMEM((ndp, cm, 16, 128), BF),
            pltpu.VMEM((ndp, nt * cm, 16, 128), BF),
            pltpu.VMEM((2, ndp, group, ds), BF),
            pltpu.VMEM((ds, ndp * group), BF),
            pltpu.VMEM((nb + 1, 16, 128), BF),
            pltpu.VMEM((nb + 1, 16, 128), BF),
            pltpu.VMEM((nb + 1, 16, 128), BF),
            pltpu.VMEM((ndp, cb, 16, ds), BF),
            pltpu.VMEM((ndp, cb, 16, ds), BF),
            pltpu.VMEM((256, 256), BF),
            dma((3,)),
            dma((2, nt // 2)),
            dma((2, nt)),
            dma((2, nt // 2)),
            dma((ndp,)),
            dma((ndp,)),
            dma((nt // 2,)),
            dma((nt,)),
            dma((nt // 4, 2)),
            dma((cb, 8)),
            dma((cb, ndp)),
            dma((cb, 8)),
            dma((cb, ndp)),
            dma((2, nt // 2)),
            dma((2, nt // 2)),
            dma((2, nt // 2)),
            dma((2, nt // 2)),
            dma((ndp,)),
            dma((ndp,)),
        ],
        compiler_params=pltpu.CompilerParams(
            collective_id=0, has_side_effects=True, vmem_limit_bytes=64 * 1024 * 1024
        ),
    )(tokens, grad_out, slot, kept, gate_blocks, up_blocks, down_blocks)
    return pl.pallas_call(
        functools.partial(hand_out, 5),
        out_shape=(own_rows, own_rows, grad, grad, grad),
        in_specs=[hb] * 5,
        out_specs=[hb] * 5,
        scratch_shapes=[pltpu.VMEM(out.shape, BF) for out in (own_rows, own_rows, grad, grad, grad)]
        + [dma((2, 5))],
    )(*results)


def solution(mesh):
    rows = P(("dp", "tensor"), None)
    blocks = P("tensor", None, None)
    grads = P("tensor", "dp", None)
    return jax.shard_map(
        on_device,
        mesh=mesh,
        in_specs=(rows, rows, P(), blocks, blocks, blocks),
        out_specs=(rows, rows, grads, grads, grads),
        check_vma=False,
    )
```

```python
import functools

import jax
import jax.numpy as jnp
from jax import lax
from jax.experimental import pallas as pl
from jax.experimental.pallas import tpu as pltpu
from jax.sharding import PartitionSpec as P

MESH = pl.DeviceIdType.MESH
BF = jnp.bfloat16
F32 = jnp.float32


def nt_dot(a, b):
    return lax.dot_general(a, b, (((1,), (1,)), ((), ())), preferred_element_type=F32)


def tn_dot(a, b):
    return lax.dot_general(a, b, (((0,), (0,)), ((), ())), preferred_element_type=F32)


def swap_matrix(outer, inner):
    n = outer * inner
    o = lax.broadcasted_iota(jnp.int32, (n, n), 0)
    i = lax.broadcasted_iota(jnp.int32, (n, n), 1)
    hit = (o // outer == i % inner) & (o % outer == i // inner)
    return jnp.where(hit, 1.0, 0.0).astype(BF)


def move(a, b):
    return jnp.dot(a, b, preferred_element_type=F32).astype(BF)


def kernel(
    dims,
    tok_ref, go_ref, slot_ref, kept_ref, gate_hbm, up_hbm, down_hbm,
    mixed_ref, gtok_ref, ggate_ref, gup_ref, gdown_ref,
    stage0, stage1, wgu, wd, own16, chunks, rows, gus, acth, actg, hid, ggu, sibx, recv, fin,
    qsend, qrecv, craw, cols, tokt, gblk, ublk, dblk, dsend, drecv, perm,
    load_sem, ag_send, ag_recv, fw_send, q_send, q_recv, cg_send, cg_recv, cf_send,
    h_send, h_recv, g_send, g_recv, sib_send, sib_recv, rs_send, rs_recv, dn_send, dn_recv,
):
    ndp, nt, m, nh, rb, cb, cap = dims
    group = m * nt
    width = nh * 2048
    ds = width // ndp
    nj = ds // 128
    nchip = nt // 2
    nz = nchip // 2
    rpd = rb // ndp
    cm = m * 2 * nj // 16
    total = ndp * group
    along_h, along_g = min(2, cb), min(1, cb)
    d = lax.axis_index("dp")
    s = lax.axis_index("tensor")
    y, x = d // 2, d % 2
    chip, core = s // 2, s % 2
    z, xh = chip // 2, chip % 2
    ny = ndp // 2

    def rdma(src, dst, ssem, rsem, dev):
        return pltpu.make_async_remote_copy(
            src_ref=src, dst_ref=dst, send_sem=ssem, recv_sem=rsem,
            device_id=dev, device_id_type=MESH,
        )

    sib = chip * 2 + (1 - core)
    xp = y * 2 + (1 - x)
    yp = lax.rem(y + 1, ny) * 2 + x
    ym = lax.rem(y + ny - 1, ny) * 2 + x
    yp_o = lax.rem(y + 1, ny) * 2 + (1 - x)
    ym_o = lax.rem(y + ny - 1, ny) * 2 + (1 - x)
    y2 = lax.rem(y + 2, ny) * 2 + x
    y2_o = lax.rem(y + 2, ny) * 2 + (1 - x)

    def chip_ahead(k):
        return lax.rem(chip + k, nchip)

    def chip_behind(k):
        return lax.rem(chip + nchip - k, nchip)

    load_g = pltpu.make_async_copy(gate_hbm, stage0.at[pl.ds(0, cap)], load_sem.at[0])
    load_u = pltpu.make_async_copy(up_hbm, stage1.at[pl.ds(0, cap)], load_sem.at[1])
    load_d = pltpu.make_async_copy(down_hbm, stage0.at[pl.ds(0, cap)], load_sem.at[2])
    barrier = pltpu.get_barrier_semaphore()
    for k in range(1, nt):
        pl.semaphore_signal(barrier, inc=1, device_id=(d, lax.rem(s + k, nt)), device_id_type=MESH)
    for k in range(1, ndp):
        pl.semaphore_signal(barrier, inc=1, device_id=(lax.rem(d + k, ndp), s), device_id_type=MESH)
    load_g.start()
    load_u.start()
    stage0[cap] = jnp.zeros((128, 128), BF)
    stage1[cap] = jnp.zeros((128, 128), BF)
    own16[...] = jnp.zeros_like(own16)
    fin[...] = jnp.zeros_like(fin)
    own16[0, 0:m, :] = tok_ref[...]
    own16[1, 0:m, :] = go_ref[...]
    perm[...] = swap_matrix(16, 16)

    for a in range(2):
        mat = jnp.concatenate(
            [
                jnp.concatenate(
                    [own16[a, :, (h * 16 + j) * 128:(h * 16 + j + 1) * 128] for j in range(16)], axis=0
                )
                for h in range(nh)
            ],
            axis=1,
        )
        out = move(perm[...], mat)
        for h in range(nh):
            chunks[a, pl.ds(s * m, m), h] = out[:, h * 128:(h + 1) * 128].reshape(16, 16, 128)[:m]
    pl.semaphore_wait(barrier, nt - 1 + ndp - 1)

    def chunk(a, src):
        return chunks.at[a, pl.ds(src * m, m)]

    def ag_copy(a, k):
        dst = chip_ahead(k) * 2 + core
        return rdma(chunk(a, s), chunk(a, s), ag_send.at[a, k], ag_recv.at[a, s], (d, dst))

    def fw_copy(a, k):
        src = chip_behind(k) * 2 + core
        return rdma(chunk(a, src), chunk(a, src), fw_send.at[a, k], ag_recv.at[a, src], (d, sib))

    def ag_arrived(a, src):
        rdma(chunk(a, src), chunk(a, src), ag_send.at[a, 0], ag_recv.at[a, src], (d, sib)).wait_recv()

    def send_own(a):
        for k in range(1, nchip):
            ag_copy(a, k).start()
        fw_copy(a, 0).start()

    send_own(0)

    def lay_inward(stage, lo):
        @pl.loop(0, rb)
        def _(r):
            for c in range(cb):
                wgu[c, pl.ds(pl.multiple_of(r * 128, 128), 128), lo:lo + 128] = stage[slot_ref[r * cb + c]]

    load_g.wait()
    lay_inward(stage0, 0)
    load_d.start()
    load_u.wait()
    send_own(1)
    lay_inward(stage1, 128)

    @pl.loop(0, ndp // 2)
    def _(pair):
        stack = jnp.concatenate(
            [own16[0, :, q * 1024:(q + 1) * 1024] for q in range(width // 1024)], axis=0
        )
        i = lax.broadcasted_iota(jnp.int32, (1024, 256), 0)
        o = lax.broadcasted_iota(jnp.int32, (1024, 256), 1) + pair * 256
        hit = (i // 128 == (o // 16) % 8) & ((i // 16) % 8 == o // 128) & (i % 16 == o % 16)
        toks = move(stack, jnp.where(hit, 1.0, 0.0).astype(BF))
        halves = []
        for w in range(2):
            base = pl.multiple_of((pair * 2 + w) * ds, 128)
            gos = jnp.concatenate(
                [own16[1, :, pl.ds(pl.multiple_of(base + j * 128, 128), 128)] for j in range(nj)], axis=0
            )
            halves.append(jnp.concatenate([toks[:, w * 128:(w + 1) * 128], gos], axis=0))
        out = move(swap_matrix(2 * nj, 16), jnp.concatenate(halves, axis=1))
        for w in range(2):
            qsend[pair * 2 + w] = out[0:cm * 16, w * 128:(w + 1) * 128].reshape(cm, 16, 128)

    def q_copy(k):
        dst = lax.rem(d + k, ndp)
        return rdma(qsend.at[dst], qrecv.at[d], q_send.at[k], q_recv.at[d], (dst, s))

    for k in range(1, ndp):
        q_copy(k).start()
    qrecv[d] = qsend[d]

    def forward(a):
        for k in range(1, nchip):
            ag_arrived(a, chip_behind(k) * 2 + core)
            fw_copy(a, k).start()

    def to_rows(a):
        @pl.loop(0, group // 16)
        def _(tb):
            t0 = pl.multiple_of(tb * 16, 16)
            mat = jnp.concatenate(
                [chunks[a, pl.ds(t0, 16), h].reshape(256, 128) for h in range(nh)], axis=1
            )
            out = move(perm[...], mat)
            for h in range(nh):
                for j in range(16):
                    lo = (h * 16 + j) * 128
                    rows[a, pl.ds(t0, 16), lo:lo + 128] = out[j * 16:(j + 1) * 16, h * 128:(h + 1) * 128]

    load_d.wait()

    @pl.loop(0, rb)
    def _(r):
        for c in range(cb):
            wd[c * 128:(c + 1) * 128, pl.ds(pl.multiple_of(r * 128, 128), 128)] = stage0[slot_ref[r * cb + c]]

    forward(0)
    for k in range(nchip):
        ag_arrived(0, chip_behind(k) * 2 + (1 - core))
    to_rows(0)

    def h_copy(c, g, n, dst):
        return rdma(acth.at[c, g], acth.at[c, g], h_send.at[c, n], h_recv.at[c, g], (dst, s))

    def h_half(c, g, part, n, dst):
        piece = acth.at[c, g, pl.ds(part * (group // 2), group // 2)]
        return rdma(piece, piece, h_send.at[c, n], h_recv.at[c, g], (dst, s))

    def g_copy(c, g, n, dst):
        return rdma(actg.at[c, g], actg.at[c, g], g_send.at[c, n], g_recv.at[c, g], (dst, s))

    def g_half(c, g, part, n, dst):
        piece = actg.at[c, g, pl.ds(part * (group // 2), group // 2)]
        return rdma(piece, piece, g_send.at[c, n], g_recv.at[c, g], (dst, s))

    @pl.loop(0, cb)
    def _(c):
        gu = jnp.dot(rows[0], wgu[c], preferred_element_type=F32)
        gus[c] = gu
        gate, up = gu[:, :128], gu[:, 128:]
        hidden = (gate * jax.nn.sigmoid(gate) * up).astype(BF)
        acth[c, d] = hidden
        h_copy(c, d, 0, xp).start()
        h_copy(c, d, 1, yp).start()
        h_copy(c, d, 2, ym).start()
        hid[:, pl.ds(pl.multiple_of(c * 128, 128), 128)] = hidden

    forward(1)
    for k in range(nchip):
        ag_arrived(1, chip_behind(k) * 2 + (1 - core))

    for k in range(1, ndp):
        src = lax.rem(d + k, ndp)
        rdma(qrecv.at[src], qrecv.at[src], q_send.at[0], q_recv.at[src], (d, sib)).wait_recv()

    def craw_of(src):
        return craw.at[:, pl.ds(src * cm, cm)]

    def at(kz, other, cr):
        along = 1 - xh if other else xh
        return (lax.rem(z + kz, nz) * 2 + along) * 2 + cr

    def cg_copy(n, dst):
        return rdma(qrecv, craw_of(s), cg_send.at[n], cg_recv.at[s], (d, dst))

    def cz_copy(k):
        src = at(0, True, core)
        return rdma(craw_of(src), craw_of(src), cg_send.at[nz + k], cg_recv.at[src], (d, at(k, False, core)))

    def cf_copy(k, other):
        src = at(k, other, core)
        return rdma(craw_of(src), craw_of(src), cf_send.at[k, other], cg_recv.at[src], (d, sib))

    def cg_arrived(src):
        rdma(craw_of(src), craw_of(src), cg_send.at[0], cg_recv.at[src], (d, sib)).wait_recv()

    cg_copy(0, sib).start()
    cg_copy(nz, at(0, True, core)).start()
    for k in range(1, nz):
        cg_copy(k, at(k, False, core)).start()
    for g in range(ndp):
        craw[g, pl.ds(s * cm, cm)] = qrecv[g]

    to_rows(1)

    @pl.loop(0, cb)
    def _(c):
        gh = nt_dot(rows[1], wd[pl.ds(pl.multiple_of(c * 128, 128), 128), :])
        gu = gus[c]
        gate, up = gu[:, :128], gu[:, 128:]
        sig = jax.nn.sigmoid(gate)
        gga = (gh * up * sig * (1.0 + gate * (1.0 - sig))).astype(BF)
        gua = (gh * (gate * sig)).astype(BF)
        actg[c, d, :, 0:128] = gga
        actg[c, d, :, 128:256] = gua
        g_copy(c, d, 0, xp).start()
        g_copy(c, d, 1, yp).start()
        g_copy(c, d, 2, ym).start()
        ggu[:, pl.ds(pl.multiple_of(c * 256, 128), 128)] = gga
        ggu[:, pl.ds(pl.multiple_of(c * 256 + 128, 128), 128)] = gua

    for a in range(2):
        for k in range(1, nchip):
            ag_copy(a, k).wait_send()
        for k in range(nchip):
            fw_copy(a, k).wait_send()
    step = min(512, width)

    def to_chunks(a):
        @pl.loop(0, group // 16)
        def _(tb):
            t0 = pl.multiple_of(tb * 16, 16)
            mat = jnp.concatenate(
                [
                    jnp.concatenate(
                        [
                            rows[a, pl.ds(t0, 16), (h * 16 + j) * 128:(h * 16 + j + 1) * 128]
                            for j in range(16)
                        ],
                        axis=0,
                    )
                    for h in range(nh)
                ],
                axis=1,
            )
            out = move(perm[...], mat)
            for h in range(nh):
                chunks[a, pl.ds(t0, 16), h] = out[:, h * 128:(h + 1) * 128].reshape(16, 16, 128)

    def sib_copy(a, q):
        return rdma(chunk(a, q * 2 + (1 - core)), sibx.at[a, q], sib_send.at[a, q], sib_recv.at[a, q], (d, sib))

    @pl.loop(along_h, cb)
    def _(c):
        h_copy(c, xp, 0, xp).wait_recv()
        h_copy(c, xp, 4, ym).start()
        h_copy(c, xp, 3, yp).start()

    cg_arrived(at(0, True, core))
    for k in range(1, nz):
        cz_copy(k).start()
    cf_copy(0, 1).start()

    @pl.loop(0, width // step)
    def _(n):
        lo = pl.multiple_of(n * step, step)
        rows[0, :, pl.ds(lo, step)] = jnp.dot(
            hid[...], wd[:, pl.ds(lo, step)], preferred_element_type=F32
        ).astype(BF)

    to_chunks(0)
    for q in range(nchip):
        sib_copy(0, q).start()

    @pl.loop(0, along_h)
    def _(c):
        h_copy(c, ym, 0, xp).wait_recv()
        h_half(c, ym, 0, 5, yp).start()
        h_copy(c, ym, 3, xp).start()
        h_copy(c, yp, 0, xp).wait_recv()
        h_half(c, yp, 1, 6, ym).start()
        h_copy(c, yp, 4, xp).start()

    @pl.loop(along_h, cb)
    def _(c):
        h_copy(c, ym, 0, xp).wait_recv()
        h_copy(c, ym, 5, yp).start()

    @pl.loop(0, width // step)
    def _(n):
        lo = pl.multiple_of(n * step, step)
        wide = jnp.concatenate([wgu[c, pl.ds(lo, step), :] for c in range(cb)], axis=1)
        rows[1, :, pl.ds(lo, step)] = nt_dot(ggu[...], wide).astype(BF)

    @pl.loop(along_g, cb)
    def _(c):
        g_copy(c, xp, 0, xp).wait_recv()
        g_copy(c, xp, 4, ym).start()
        g_copy(c, xp, 3, yp).start()

    to_chunks(1)
    for q in range(nchip):
        sib_copy(1, q).start()

    @pl.loop(0, along_h)
    def _(c):
        h_copy(c, y2, 0, xp).wait_recv()
        h_copy(c, y2, 7, xp).start()

    @pl.loop(along_h, cb)
    def _(c):
        h_copy(c, yp_o, 0, xp).wait_recv()
        h_copy(c, yp_o, 6, ym).start()

    def rs_copy(a, k):
        q = chip_ahead(k)
        return rdma(
            chunk(a, q * 2 + core), recv.at[a, chip], rs_send.at[a, k], rs_recv.at[a, chip], (d, q * 2 + core)
        )

    for a in range(2):
        for q in range(nchip):
            sib_copy(a, q).wait_recv()
        for k in range(nchip):
            q = chip_ahead(k)
            mine = pl.ds((q * 2 + core) * m, m)
            both = (chunks[a, mine].astype(F32) + sibx[a, q].astype(F32)).astype(BF)
            if k == 0:
                recv[a, chip] = both
            else:
                chunks[a, mine] = both
                rs_copy(a, k).start()

    @pl.loop(0, along_g)
    def _(c):
        g_copy(c, ym, 0, xp).wait_recv()
        g_half(c, ym, 0, 5, yp).start()
        g_copy(c, ym, 3, xp).start()
        g_copy(c, yp, 0, xp).wait_recv()
        g_half(c, yp, 1, 6, ym).start()
        g_copy(c, yp, 4, xp).start()

    @pl.loop(along_g, cb)
    def _(c):
        g_copy(c, ym, 0, xp).wait_recv()
        g_copy(c, ym, 5, yp).start()

    for k in range(1, nz):
        for other in range(2):
            cg_arrived(at(k, other, core))
            cf_copy(k, other).start()
    for k in range(nz):
        for other in range(2):
            cg_arrived(at(k, other, 1 - core))

    @pl.loop(0, ndp // 2)
    def _(gp):
        for tb in range(group // 32):
            per = 32 * 2 * nj // 16
            mat = jnp.concatenate(
                [craw[gp * 2 + w, tb * per:(tb + 1) * per].reshape(per * 16, 128) for w in range(2)], axis=1
            )
            out = move(swap_matrix(32, 2 * nj), mat)
            for w in range(2):
                for a in range(2):
                    for j in range(nj):
                        lo = (a * nj + j) * 32
                        cols[a, gp * 2 + w, tb * 32:(tb + 1) * 32, j * 128:(j + 1) * 128] = (
                            out[lo:lo + 32, w * 128:(w + 1) * 128]
                        )

    tall = cols[0].reshape(total, ds)
    for q in range(total // 128):
        tokt[:, q * 128:(q + 1) * 128] = tall[q * 128:(q + 1) * 128].T

    @pl.loop(0, along_g)
    def _(c):
        g_copy(c, y2, 0, xp).wait_recv()
        g_copy(c, y2, 7, xp).start()

    @pl.loop(along_g, cb)
    def _(c):
        g_copy(c, yp_o, 0, xp).wait_recv()
        g_copy(c, yp_o, 6, ym).start()

    def dn_copy(c, k):
        dst = lax.rem(d + k, ndp)
        return rdma(dsend.at[dst, c], drecv.at[d, c], dn_send.at[k], dn_recv.at[d], (dst, s))

    def grad_down(c):
        down = tn_dot(acth[c].reshape(total, 128), cols[1].reshape(total, ds)).astype(BF)
        for o in range(ndp):
            dsend[o, c] = down[o * 16:(o + 1) * 16]
        for k in range(1, ndp):
            dn_copy(c, k).start()
        drecv[d, c] = dsend[d, c]

    @pl.loop(0, along_h)
    def _(c):
        for g in (xp, ym_o, yp_o, y2_o):
            h_copy(c, g, 0, xp).wait_recv()
        grad_down(c)

    @pl.loop(along_h, cb)
    def _(c):
        for g in (ym_o, yp, y2, y2_o):
            h_copy(c, g, 0, xp).wait_recv()
        grad_down(c)

    for a, out_ref in ((0, mixed_ref), (1, gtok_ref)):
        for k in range(1, nchip):
            q = chip_ahead(k)
            rdma(recv.at[a, q], recv.at[a, q], rs_send.at[a, 0], rs_recv.at[a, q], (d, sib)).wait_recv()
        fin[0:m] = jnp.sum(recv[a].astype(F32), axis=0).astype(BF)
        mat = jnp.concatenate([fin[:, h].reshape(256, 128) for h in range(nh)], axis=1)
        out = move(perm[...], mat)
        for h in range(nh):
            for j in range(16):
                lo = (h * 16 + j) * 128
                out_ref[:, lo:lo + 128] = out[j * 16:j * 16 + m, h * 128:(h + 1) * 128]

    def grad_inward(c):
        both = jnp.dot(tokt[...], actg[c].reshape(total, 256), preferred_element_type=F32).astype(BF)
        for r in range(rb):
            gblk[r * cb + c] = both[r * 16:(r + 1) * 16, :128]
            ublk[r * cb + c] = both[r * 16:(r + 1) * 16, 128:]

    @pl.loop(0, along_g)
    def _(c):
        for g in (xp, ym_o, yp_o, y2_o):
            g_copy(c, g, 0, xp).wait_recv()
        grad_inward(c)

    @pl.loop(along_g, cb)
    def _(c):
        for g in (ym_o, yp, y2, y2_o):
            g_copy(c, g, 0, xp).wait_recv()
        grad_inward(c)

    zero = jnp.zeros((16, 128), BF)
    gblk[rb * cb] = zero
    ublk[rb * cb] = zero
    dblk[rb * cb] = zero

    for k in range(1, ndp):
        src = lax.rem(d + k, ndp)
        rdma(drecv.at[src], drecv.at[src], dn_send.at[0], dn_recv.at[src], (d, sib)).wait_recv()
    for r in range(rb):
        for c in range(cb):
            lo = (r % rpd) * 128
            dblk[r * cb + c] = drecv[r // rpd, c, :, lo:lo + 128]

    @pl.loop(0, cap)
    def _(k):
        ggate_ref[k] = gblk[kept_ref[k]]
        gup_ref[k] = ublk[kept_ref[k]]
        gdown_ref[k] = dblk[kept_ref[k]]

    for k in range(1, ndp):
        q_copy(k).wait_send()
        rdma(dsend.at[lax.rem(d + k, ndp)], drecv.at[d], dn_send.at[k], dn_recv.at[d], (d, sib)).wait_send()
    cg_copy(0, sib).wait_send()
    cg_copy(nz, sib).wait_send()
    cf_copy(0, 1).wait_send()
    for k in range(1, nz):
        cg_copy(k, sib).wait_send()
        cz_copy(k).wait_send()
        for other in range(2):
            cf_copy(k, other).wait_send()
    for a in range(2):
        for q in range(nchip):
            sib_copy(a, q).wait_send()
        for k in range(1, nchip):
            rs_copy(a, k).wait_send()

    @pl.loop(0, along_h)
    def _(c):
        for n, g in ((0, d), (1, d), (2, d), (3, ym), (4, yp), (7, y2)):
            h_copy(c, g, n, xp).wait_send()
        for n, g in ((5, ym), (6, yp)):
            h_half(c, g, 0, n, xp).wait_send()

    @pl.loop(along_h, cb)
    def _(c):
        for n, g in enumerate((d, d, d, xp, xp, ym, yp_o)):
            h_copy(c, g, n, xp).wait_send()

    @pl.loop(0, along_g)
    def _(c):
        for n, g in ((0, d), (1, d), (2, d), (3, ym), (4, yp), (7, y2)):
            g_copy(c, g, n, xp).wait_send()
        for n, g in ((5, ym), (6, yp)):
            g_half(c, g, 0, n, xp).wait_send()

    @pl.loop(along_g, cb)
    def _(c):
        for n, g in enumerate((d, d, d, xp, xp, ym, yp_o)):
            g_copy(c, g, n, xp).wait_send()


def hand_out(n, *refs):
    given, results, held, sems = refs[:n], refs[n:2 * n], refs[2 * n:3 * n], refs[3 * n]
    loads = [pltpu.make_async_copy(given[i], held[i], sems.at[0, i]) for i in range(n)]
    stores = [pltpu.make_async_copy(held[i], results[i], sems.at[1, i]) for i in range(n)]
    for load in loads:
        load.start()
    for load, store in zip(loads, stores):
        load.wait()
        store.start()
    for store in stores:
        store.wait()


def on_device(tokens, grad_out, block_mask, gate_blocks, up_blocks, down_blocks):
    nt = lax.axis_size("tensor")
    ndp = lax.axis_size("dp")
    shard = lax.axis_index("tensor")
    rb = block_mask.shape[0]
    cb = block_mask.shape[1] // nt
    cap = gate_blocks.shape[0]
    m, width = tokens.shape
    nh = width // 2048
    group = m * nt
    ds = width // ndp
    nb = rb * cb
    cm = m * 2 * (ds // 128) // 16
    flags = lax.dynamic_slice_in_dim(block_mask, shard * cb, cb, 1).reshape(-1)
    pos = jnp.arange(nb, dtype=jnp.int32)
    upto = jnp.sum(jnp.where(pos[None, :] <= pos[:, None], flags[None, :], 0), axis=1)
    slot = jnp.where(flags > 0, upto - 1, cap)
    kept = jnp.sum((upto[None, :] <= jnp.arange(cap, dtype=jnp.int32)[:, None]).astype(jnp.int32), axis=1)

    vm = pl.BlockSpec(memory_space=pltpu.VMEM)
    sm = pl.BlockSpec(memory_space=pltpu.SMEM)
    hb = pl.BlockSpec(memory_space=pl.ANY)
    dma = pltpu.SemaphoreType.DMA
    own_rows = jax.ShapeDtypeStruct((m, width), BF)
    grad = jax.ShapeDtypeStruct((cap, 16, 128), BF)
    results = pl.pallas_call(
        functools.partial(kernel, (ndp, nt, m, nh, rb, cb, cap)),
        out_shape=(own_rows, own_rows, grad, grad, grad),
        in_specs=[vm, vm, sm, sm, hb, hb, hb],
        out_specs=[vm] * 5,
        scratch_shapes=[
            pltpu.VMEM((cap + 1, 128, 128), BF),
            pltpu.VMEM((cap + 1, 128, 128), BF),
            pltpu.VMEM((cb, width, 256), BF),
            pltpu.VMEM((cb * 128, width), BF),
            pltpu.VMEM((2, 16, width), BF),
            pltpu.VMEM((2, group, nh, 16, 128), BF),
            pltpu.VMEM((2, group, width), BF),
            pltpu.VMEM((cb, group, 256), F32),
            pltpu.VMEM((cb, ndp, group, 128), BF),
            pltpu.VMEM((cb, ndp, group, 256), BF),
            pltpu.VMEM((group, cb * 128), BF),
            pltpu.VMEM((group, cb * 256), BF),
            pltpu.VMEM((2, nt // 2, m, nh, 16, 128), BF),
            pltpu.VMEM((2, nt // 2, m, nh, 16, 128), BF),
            pltpu.VMEM((16, nh, 16, 128), BF),
            pltpu.VMEM((ndp, cm, 16, 128), BF),
            pltpu.VMEM((ndp, cm, 16, 128), BF),
            pltpu.VMEM((ndp, nt * cm, 16, 128), BF),
            pltpu.VMEM((2, ndp, group, ds), BF),
            pltpu.VMEM((ds, ndp * group), BF),
            pltpu.VMEM((nb + 1, 16, 128), BF),
            pltpu.VMEM((nb + 1, 16, 128), BF),
            pltpu.VMEM((nb + 1, 16, 128), BF),
            pltpu.VMEM((ndp, cb, 16, ds), BF),
            pltpu.VMEM((ndp, cb, 16, ds), BF),
            pltpu.VMEM((256, 256), BF),
            dma((3,)),
            dma((2, nt // 2)),
            dma((2, nt)),
            dma((2, nt // 2)),
            dma((ndp,)),
            dma((ndp,)),
            dma((nt // 2,)),
            dma((nt,)),
            dma((nt // 4, 2)),
            dma((cb, 8)),
            dma((cb, ndp)),
            dma((cb, 8)),
            dma((cb, ndp)),
            dma((2, nt // 2)),
            dma((2, nt // 2)),
            dma((2, nt // 2)),
            dma((2, nt // 2)),
            dma((ndp,)),
            dma((ndp,)),
        ],
        compiler_params=pltpu.CompilerParams(
            collective_id=0, has_side_effects=True, vmem_limit_bytes=64 * 1024 * 1024
        ),
    )(tokens, grad_out, slot, kept, gate_blocks, up_blocks, down_blocks)
    return pl.pallas_call(
        functools.partial(hand_out, 5),
        out_shape=(own_rows, own_rows, grad, grad, grad),
        in_specs=[hb] * 5,
        out_specs=[hb] * 5,
        scratch_shapes=[pltpu.VMEM(out.shape, BF) for out in (own_rows, own_rows, grad, grad, grad)]
        + [dma((2, 5))],
    )(*results)


def solution(mesh):
    rows = P(("dp", "tensor"), None)
    blocks = P("tensor", None, None)
    grads = P("tensor", "dp", None)
    return jax.shard_map(
        on_device,
        mesh=mesh,
        in_specs=(rows, rows, P(), blocks, blocks, blocks),
        out_specs=(rows, rows, grads, grads, grads),
        check_vma=False,
    )
```
